32 devices in a mesh: grp: 2 (over x), idx: 16 (over z, y, core).
Axes of the slice: x: 2, y: 2, z: 4, core: 2. Of those that a mesh axis runs over, the one named last changes fastest.
Arguments:
- amplitudes: bfloat16 [256, 80000], P(('grp', 'idx')), parts along dimension 0, may hold values from -0.109375 to 0.109375
- integrals: bfloat16 [256, 80000], P(('grp', 'idx')), parts along dimension 0, may hold values from -8 to 8
- hole_integrals: bfloat16 [32, 8, 16], P(('grp', 'idx')), parts along dimension 0, may hold values from -24 to 24
- occ_energy: float32 [400], P('grp'), parts along dimension 0, may hold values from -2 to -0.3
- vir_energy: float32 [1600], P('grp'), parts along dimension 0, may hold values from 0.2 to 3
- pair_orbitals: int32 [256, 2], P(('grp', 'idx')), parts along dimension 0, may hold values from 0 to 199
Outputs:
- new_amplitudes: bfloat16 [256, 80000], P(('grp', 'idx')), parts along dimension 0
The draws below stay inside these ranges and needn't reach their ends.
There are 2 independent parts, one for each index of `grp`. The reference program is written for one: setup_inputs(seed, part) draws one part's arguments, and reference() takes and returns one part's arrays. A program takes and returns all parts, laid end to end along the dimension named above; each array names one. Nothing has to cross between parts.
All inputs are finite; a program needn't handle non-finite values.
Results may differ from the reference program's by a relative error of at most 0.0034.
Values may be sent and summed in bfloat16 or wider, within the bound.
No kernel may reach another device: no remote copies, remote signals or barrier semaphores. Data moves between devices by JAX's collectives and lax.ppermute only.
A program may use at most 64 MiB of HBM per device.

```python
import jax
import jax.numpy as jnp
from jax import lax

IRREPS = 8
BS = 100
OCC = 200
VIR = 800
TILE = 80000
PAIRS = 128
PAIRS_SYM = 16


def with_ends(values, rng, least, largest):
    extent = values.shape
    index_at = [jax.random.randint(jax.random.fold_in(rng, axis), (), 0, extent[axis]) for axis in range(len(extent))]
    values = values.at[tuple(index_at)].set(least)
    longest = extent.index(max(extent))
    index_at[longest] = (index_at[longest] + 1) % extent[longest]
    return values.at[tuple(index_at)].set(largest)


def raised(array, key, source, target, blocks, factor):
    def block_of(dim):
        return (jnp.arange(array.shape[dim]) // (array.shape[dim] // blocks)).reshape((-1,) + (1,) * (array.ndim - 1 - dim))

    one_side = jax.random.permutation(key, blocks)[block_of(target)]
    other_side = (block_of(target) + blocks // 2) % blocks
    return jnp.where((block_of(source) == one_side) | (block_of(source) == other_side), factor * array, array)


def block_scale(own_key, shape, pieces, smallest, top_value):
    def one(position, parts):
        heights = jax.random.uniform(jax.random.fold_in(jax.random.fold_in(own_key, 6), position), (parts,), jnp.float32, smallest / len(pieces), top_value / len(pieces))
        return jnp.repeat(jnp.exp(heights), shape[position] // parts).reshape((-1,) + (1,) * (len(shape) - position - 1))

    level = one(*pieces[0])
    for cut in pieces[1:]:
        level = level * one(*cut)
    return level


def bell_draw(rng, shape, scale, most, cuts=(), kind=jnp.bfloat16):
    values = jax.random.normal(rng, shape, jnp.float32) * scale
    if len(cuts) > 0:
        values = block_scale(rng, shape, cuts, -0.22, 0.18) * values
    return jnp.clip(values, min=-most, max=most).astype(kind)


def bell_draw_with(own_key, shape, deviation, reach, cuts, heavy, kind=jnp.bfloat16):
    drawn = deviation * jax.random.normal(own_key, shape, jnp.float32)
    if cuts:
        drawn = drawn * block_scale(own_key, shape, cuts, -0.22, 0.18)
    return jnp.clip(raised(drawn, jax.random.fold_in(own_key, 3), *heavy), -reach, reach).astype(kind)


def setup_inputs(seed: int = 0, part: int = 0) -> dict:
    arg_keys = jax.random.split(jax.random.key(seed), 7)
    part_splits = jax.random.split(jax.random.fold_in(arg_keys[6], part), 7)
    amplitudes = bell_draw(part_splits[0], (PAIRS, TILE), (2.0 / TILE ** 0.5), 0.109375, ((0, 16),))
    integrals = bell_draw_with(part_splits[1], (PAIRS, TILE), 2.0, 8.0, ((0, 16),), (1, 0, 16, 2.0))
    hole_integrals = bell_draw(part_splits[2], (PAIRS_SYM, IRREPS, PAIRS_SYM), 4.0, 24.0, ((0, 16),))
    occ_energy = jnp.clip(jax.random.uniform(part_splits[3], (OCC,), jnp.float32, -2.0, -0.3), -2.0, -0.3)
    vir_energy = jnp.clip(jax.random.uniform(part_splits[4], (VIR,), jnp.float32, 0.2, 3.0), 0.2, 3.0)
    pair_orbitals = with_ends(jax.random.randint(part_splits[5], (PAIRS, 2), 0, OCC), jax.random.fold_in(part_splits[5], 1), 0, OCC - 1).astype(jnp.int32)
    return dict(amplitudes=amplitudes, integrals=integrals, hole_integrals=hole_integrals, occ_energy=occ_energy, vir_energy=vir_energy, pair_orbitals=pair_orbitals)


def reference(amplitudes, integrals, hole_integrals, occ_energy, vir_energy, pair_orbitals):
    vir_blocks = vir_energy.reshape(IRREPS, BS)
    sym_ids = jnp.arange(IRREPS, dtype=jnp.int32)
    partner = jnp.bitwise_xor(sym_ids[:, None], sym_ids[None, :])
    partner_energy = vir_blocks[partner]
    amp_blocks = amplitudes.reshape(IRREPS, PAIRS_SYM, TILE)
    int_blocks = integrals.reshape(IRREPS, PAIRS_SYM, TILE)
    bare_blocks = jnp.transpose(hole_integrals, (1, 0, 2))
    orbital_blocks = pair_orbitals.reshape(IRREPS, PAIRS_SYM, 2)

    def one_symmetry(inputs):
        amps_sym, ints_sym, bare_sym, orbitals_sym, energy_partner = inputs
        chi = bare_sym.astype(jnp.float32) + jnp.dot(amps_sym, ints_sym.T, preferred_element_type=jnp.float32)
        chi_half = chi.astype(jnp.bfloat16)
        ladder = jnp.dot(chi_half, amps_sym, preferred_element_type=jnp.float32).astype(jnp.bfloat16)
        ladder = lax.optimization_barrier(ladder)
        occupied = occ_energy[orbitals_sym[:, 0]] + occ_energy[orbitals_sym[:, 1]]
        denom = vir_blocks[None, :, :, None] + energy_partner[None, :, None, :] - occupied[:, None, None, None]
        total = ints_sym.astype(jnp.float32) + ladder.astype(jnp.float32)
        return (total / denom.reshape(PAIRS_SYM, TILE)).astype(jnp.bfloat16)

    result = lax.map(one_symmetry, (amp_blocks, int_blocks, bare_blocks, orbital_blocks, partner_energy))
    return result.reshape(PAIRS, TILE)
```

```python
import jax
import jax.numpy as jnp
from jax import lax
from jax.sharding import PartitionSpec as P

IRREPS = 8


def team_exchange(block, team, size):
    return [
        lax.ppermute(block, "idx", [(d, (d // team) * team + (d - step) % team) for d in range(size)])
        for step in range(1, team)
    ]


def reciprocal_denominators(occ_energy, vir_energy, pair_orbitals, symmetry):
    sym_ids = jnp.arange(IRREPS, dtype=jnp.int32)
    vir_blocks = vir_energy.reshape(IRREPS, -1)
    partner = jnp.bitwise_xor(symmetry, sym_ids)
    onehot = (partner[:, None] == sym_ids[None, :]).astype(jnp.float32)
    energy_partner = jnp.einsum("gh,hb->gb", onehot, vir_blocks, precision=lax.Precision.HIGHEST)
    virtual = (vir_blocks[:, :, None] + energy_partner[:, None, :]).reshape(-1)
    orbital_ids = jnp.arange(occ_energy.shape[0], dtype=jnp.int32)
    occ_onehot = pair_orbitals[:, :, None] == orbital_ids[None, None, :]
    occ_each = jnp.sum(jnp.where(occ_onehot, occ_energy[None, None, :], 0.0), axis=-1)
    occupied = occ_each[:, 0] + occ_each[:, 1]
    return 1.0 / (virtual[None, :] - occupied[:, None])


def on_device(amplitudes, integrals, hole_integrals, occ_energy, vir_energy, pair_orbitals, size):
    local_pairs = amplitudes.shape[0]
    pair_count = local_pairs * size // IRREPS
    team = pair_count // local_pairs
    me = lax.axis_index("idx")
    symmetry, rank = me // team, me % team

    amps = [amplitudes] + team_exchange(amplitudes, team, size)
    ints = [integrals] + team_exchange(integrals, team, size)

    bare = jnp.repeat(jnp.swapaxes(hole_integrals, 0, 1), team, axis=0)
    bare = lax.all_to_all(bare, "idx", split_axis=0, concat_axis=0, tiled=True)
    bare = bare.reshape(pair_count, pair_count)
    bare = lax.dynamic_slice_in_dim(bare, rank * local_pairs, local_pairs, axis=0)
    bare = bare.reshape(local_pairs, team, local_pairs).astype(jnp.float32)

    inverse = reciprocal_denominators(occ_energy, vir_energy, pair_orbitals, symmetry)
    ladder = 0.0
    for step in range(team):
        chi = jnp.einsum("ie,ke->ik", amplitudes, ints[step], preferred_element_type=jnp.float32)
        mine = lax.dynamic_index_in_dim(bare, (rank + step) % team, axis=1, keepdims=False)
        chi_half = (mine + chi).astype(jnp.bfloat16)
        ladder += jnp.einsum("ik,ke->ie", chi_half, amps[step], preferred_element_type=jnp.float32)
    total = integrals.astype(jnp.float32) + ladder.astype(jnp.bfloat16).astype(jnp.float32)
    return (total * inverse).astype(jnp.bfloat16)


def solution(mesh):
    size = mesh.shape["idx"]
    in_specs = (
        P(("grp", "idx"), None),
        P(("grp", "idx"), None),
        P(("grp", "idx"), None, None),
        P("grp"),
        P("grp"),
        P(("grp", "idx"), None),
    )
    out_specs = P(("grp", "idx"), None)

    def run(*args):
        return on_device(*args, size)

    return jax.shard_map(run, mesh=mesh, in_specs=in_specs, out_specs=out_specs, check_vma=False)
```

```python
import functools

import jax
import jax.numpy as jnp
import numpy as np
from jax import lax
from jax.experimental import pallas as pl
from jax.experimental.pallas import tpu as pltpu
from jax.sharding import PartitionSpec as P

IRREPS = 8
CHUNKS = 5
IN_VMEM = pl.BlockSpec(memory_space=pltpu.VMEM)
PARAMS = pltpu.CompilerParams(vmem_limit_bytes=24 * 1024 * 1024)


def chunk_slices(width):
    tiles = width // 128
    edges = [tiles * c // CHUNKS * 128 for c in range(CHUNKS)] + [width]
    return [pl.ds(start, stop - start) for start, stop in zip(edges, edges[1:])]


def chi_kernel(team, amps_ref, *refs):
    ints, chi_ref = refs[:team], refs[team]
    total = jnp.zeros(chi_ref.shape, jnp.float32)
    for cut in chunk_slices(amps_ref.shape[1]):
        columns = jnp.concatenate([ref[:, cut] for ref in ints], axis=0)
        total += lax.dot_general(
            amps_ref[:, cut], columns, (((1,), (1,)), ((), ())), preferred_element_type=jnp.float32
        )
    chi_ref[...] = total


def update_kernel(team, slabs, rows_ref, order_ref, chi_ref, virtual_ref, occupied_ref, ints_ref, *refs):
    bare, amps = refs[:slabs], refs[slabs : slabs + team]
    out_ref, buffer, sems = refs[slabs + team :]
    stack = jnp.concatenate([ref[...] for ref in bare], axis=0)
    pairs, count = chi_ref.shape
    pick = lax.broadcasted_iota(jnp.int32, (pairs, stack.shape[0]), 1) == rows_ref[...]
    mine = jnp.dot(pick.astype(jnp.bfloat16), stack, preferred_element_type=jnp.float32)
    turn = lax.broadcasted_iota(jnp.int32, (count, count), 0) == order_ref[...]
    mine = jnp.dot(mine.astype(jnp.bfloat16), turn.astype(jnp.bfloat16), preferred_element_type=jnp.float32)
    chi_half = (mine + chi_ref[...]).astype(jnp.bfloat16)
    copies = []
    for index, cut in enumerate(chunk_slices(ints_ref.shape[1])):
        block = jnp.concatenate([ref[:, cut] for ref in amps], axis=0)
        ladder = jnp.dot(chi_half, block, preferred_element_type=jnp.float32).astype(jnp.bfloat16)
        total = ints_ref[:, cut].astype(jnp.float32) + ladder.astype(jnp.float32)
        denominator = virtual_ref[:, cut] - occupied_ref[...]
        buffer[:, cut] = (total / denominator).astype(jnp.bfloat16)
        copy = pltpu.make_async_copy(buffer.at[:, cut], out_ref.at[:, cut], sems.at[index])
        copy.start()
        copies.append(copy)
    for copy in copies:
        copy.wait()


def team_exchange(block, team, size):
    return [
        lax.ppermute(block, "idx", [(d, (d // team) * team + (d - step) % team) for d in range(size)])
        for step in range(1, team)
    ]


def exchange_rows_16(hole):
    near, far, both = 6, 4, 2

    def home(d):
        return (d >> 3) == (d & 1)

    hops = (
        [(d, d ^ (near if home(d) else far ^ 9)) for d in range(16)],
        [(d, d ^ (both if home(d) else both ^ 9)) for d in range(16)],
        [(d, d ^ 8) for d in range(16)],
    )
    own = jnp.concatenate([hole, lax.ppermute(hole, "idx", [(d, d ^ 1) for d in range(16)])], axis=0)
    first = lax.ppermute(own, "idx", hops[0])
    second = lax.ppermute(own, "idx", hops[1])
    third = lax.ppermute(jnp.concatenate([own, first], axis=0), "idx", hops[2])

    def held(d):
        return [d, d ^ 1]

    source = [dict((dst, src) for src, dst in hop) for hop in hops]
    table = np.zeros((16, 8), np.int32)
    for d in range(16):
        one, two, three = (hop[d] for hop in source)
        slots = held(d) + held(one) + held(two) + held(three) + held(source[0][three])
        table[d] = [slots.index((d & 1) * 8 + row) for row in range(8)]
    return [own, first, second, third], table


def exchange_rows(hole, team, size):
    rows, _, count = hole.shape
    sent = jnp.repeat(jnp.swapaxes(hole, 0, 1), team, axis=0)
    received = lax.all_to_all(sent, "idx", split_axis=0, concat_axis=0, tiled=True)
    table = np.arange(count, dtype=np.int32).reshape(team, -1)[np.arange(size) % team]
    return [received.reshape(size * rows, 1, count)], table


def virtual_sums(vir_energy, symmetry):
    sym_ids = jnp.arange(IRREPS, dtype=jnp.int32)
    blocks = vir_energy.reshape(IRREPS, -1)
    onehot = (jnp.bitwise_xor(symmetry, sym_ids)[:, None] == sym_ids[None, :]).astype(jnp.float32)
    partner = jnp.einsum("gh,hb->gb", onehot, blocks, precision=lax.Precision.HIGHEST)
    return (blocks[:, :, None] + partner[:, None, :]).reshape(1, -1)


def occupied_sums(occ_energy, pair_orbitals):
    orbital_ids = jnp.arange(occ_energy.shape[0], dtype=jnp.int32)
    onehot = pair_orbitals[:, :, None] == orbital_ids[None, None, :]
    each = jnp.sum(jnp.where(onehot, occ_energy[None, None, :], 0.0), axis=-1)
    return each[:, 0:1] + each[:, 1:2]


def on_device(amplitudes, integrals, hole_integrals, occ_energy, vir_energy, pair_orbitals, size):
    local_pairs, width = amplitudes.shape
    pair_count = hole_integrals.shape[2]
    team = pair_count // local_pairs
    me = lax.axis_index("idx")
    symmetry, rank = me // team, me % team

    if size == 16 and team == 2:
        slabs, table = exchange_rows_16(hole_integrals)
    else:
        slabs, table = exchange_rows(hole_integrals, team, size)
    amps = [amplitudes] + team_exchange(amplitudes, team, size)
    ints = [integrals] + team_exchange(integrals, team, size)

    wide = slabs[0].shape[1]
    slabs = [slab.reshape(-1, pair_count) for slab in slabs]
    rows = lax.dynamic_slice_in_dim(jnp.asarray(table), me, 1, axis=0).reshape(local_pairs, 1)
    if wide > 1:
        rows = rows * wide + symmetry
    order = (jnp.arange(pair_count, dtype=jnp.int32) + rank * local_pairs) % pair_count

    chi = pl.pallas_call(
        functools.partial(chi_kernel, team),
        out_shape=jax.ShapeDtypeStruct((local_pairs, pair_count), jnp.float32),
        in_specs=[IN_VMEM] * (1 + team),
        out_specs=IN_VMEM,
        compiler_params=PARAMS,
        cost_estimate=pl.CostEstimate(
            flops=2 * local_pairs * pair_count * width, bytes_accessed=2 * local_pairs * width * 2, transcendentals=0
        ),
    )(amplitudes, *ints)
    return pl.pallas_call(
        functools.partial(update_kernel, team, len(slabs)),
        out_shape=jax.ShapeDtypeStruct((local_pairs, width), jnp.bfloat16),
        in_specs=[IN_VMEM] * (6 + len(slabs) + team),
        out_specs=pl.BlockSpec(memory_space=pl.ANY),
        scratch_shapes=[
            pltpu.VMEM((local_pairs, width), jnp.bfloat16),
            pltpu.SemaphoreType.DMA((CHUNKS,)),
        ],
        compiler_params=PARAMS,
        cost_estimate=pl.CostEstimate(
            flops=2 * local_pairs * pair_count * width, bytes_accessed=4 * local_pairs * width * 2, transcendentals=0
        ),
    )(
        rows,
        order.reshape(1, pair_count),
        chi,
        virtual_sums(vir_energy, symmetry),
        occupied_sums(occ_energy, pair_orbitals),
        integrals,
        *slabs,
        *amps,
    )


def solution(mesh):
    size = mesh.shape["idx"]
    in_specs = (
        P(("grp", "idx"), None),
        P(("grp", "idx"), None),
        P(("grp", "idx"), None, None),
        P("grp"),
        P("grp"),
        P(("grp", "idx"), None),
    )
    out_specs = P(("grp", "idx"), None)

    def run(*args):
        return on_device(*args, size)

    return jax.shard_map(run, mesh=mesh, in_specs=in_specs, out_specs=out_specs, check_vma=False)
```

```python
import functools
import math

import jax
import jax.numpy as jnp
from jax import lax
from jax.experimental import pallas as pl
from jax.experimental.pallas import tpu as pltpu
from jax.sharding import PartitionSpec as P

IRREPS = 8
CHUNKS = 5
IN_VMEM = pl.BlockSpec(memory_space=pltpu.VMEM)


def cuts(width, period):
    count = width // period
    edges = [count * c // CHUNKS for c in range(CHUNKS + 1)]
    return [(edge, stop) for edge, stop in zip(edges, edges[1:]) if stop > edge]


def one_hot_sum(values, columns):
    lanes = lax.broadcasted_iota(jnp.int32, (columns.shape[0], values.shape[1]), 1)
    return jnp.sum(jnp.where(lanes == columns, values, 0.0), axis=1, keepdims=True)


def occupied_sums(occ, orbitals):
    pairs = orbitals.shape[1]
    diagonal = lax.broadcasted_iota(jnp.int32, (pairs, pairs), 0) == lax.broadcasted_iota(
        jnp.int32, (pairs, pairs), 1
    )
    each = [
        one_hot_sum(occ, jnp.sum(jnp.where(diagonal, orbitals[j : j + 1, :], 0), axis=1, keepdims=True))
        for j in range(2)
    ]
    return jnp.broadcast_to(each[0] + each[1], (pairs, 128))


def virtual_sums(vir, symmetry, rows, period):
    block = vir.shape[1] // IRREPS
    step = period // block
    padded = jnp.concatenate([vir, jnp.zeros((1, 128), jnp.float32)], axis=1)
    held = -(-rows // 8) * 8
    row = lax.broadcasted_iota(jnp.int32, (held, 128), 0)
    lane = lax.broadcasted_iota(jnp.int32, (held, 128), 1)

    def irrep_of(orbital):
        return sum((orbital >= block * q).astype(jnp.int32) for q in range(1, IRREPS))

    def partner(orbital):
        other = jnp.bitwise_xor(irrep_of(orbital), symmetry)
        energies = jnp.zeros((held, 128), jnp.float32)
        for q in range(IRREPS):
            energies = jnp.where(other == q, padded[:, block * q : block * q + 128], energies)
        return energies

    firsts = [padded[:, step * r : step * r + 128] for r in range(rows)]
    first = jnp.concatenate(firsts + [jnp.zeros((held - rows, 128), jnp.float32)], axis=0)
    low, high = partner(row * step), partner(row * step + step - 1)
    turn = (irrep_of(row * step) + 1) * block
    sums = []
    for tile in range(period // 128):
        start = tile * 128 // block
        element = lane + tile * 128
        a = start + sum((element >= block * (start + q)).astype(jnp.int32) for q in range(1, 2 + 127 // block))
        b = element - a * block
        second = jnp.where(
            row * step + a >= turn, jnp.take_along_axis(high, b, axis=1), jnp.take_along_axis(low, b, axis=1)
        )
        sums.append(jnp.take_along_axis(first, a, axis=1) + second)
    return jnp.concatenate(sums, axis=1)


def chi_kernel(team, rows, vir_ref, occ_ref, orbitals_ref, amps_ref, *refs):
    ints, (chi_ref, virtual_ref, occupied_ref) = refs[:team], refs[team:]
    symmetry = lax.axis_index("idx") // team
    period = virtual_ref.shape[1]
    total = jnp.zeros(chi_ref.shape, jnp.float32)
    for start, stop in cuts(amps_ref.shape[1], period):
        cut = pl.ds(start * period, (stop - start) * period)
        columns = jnp.concatenate([ref[:, cut] for ref in ints], axis=0)
        total += lax.dot_general(
            amps_ref[:, cut], columns, (((1,), (1,)), ((), ())), preferred_element_type=jnp.float32
        )
    chi_ref[...] = total
    virtual_ref[...] = virtual_sums(vir_ref[...], symmetry, rows, period)
    occupied_ref[...] = occupied_sums(occ_ref[...], orbitals_ref[...])


def update_kernel(team, slabs, owners, chi_ref, virtual_ref, occupied_ref, ints_ref, *refs):
    bare, amps = refs[:slabs], refs[slabs : slabs + team]
    out_ref, buffer, sems = refs[slabs + team :]
    me = lax.axis_index("idx")
    symmetry, rank = me // team, me % team
    pairs, count = chi_ref.shape
    stack = jnp.concatenate([ref[...] for ref in bare], axis=0)
    held = owners(me)
    lane = lax.broadcasted_iota(jnp.int32, (pairs, stack.shape[0]), 1)
    if held is None:
        owner = lane
    else:
        wide = stack.shape[0] // len(held)
        owner = jnp.full(lane.shape, -1, jnp.int32)
        for slot, row in enumerate(held):
            owner = jnp.where(lane == slot * wide + symmetry, row, owner)
    pick = owner == rank * pairs + lax.broadcasted_iota(jnp.int32, lane.shape, 0)
    mine = jnp.dot(pick.astype(jnp.bfloat16), stack, preferred_element_type=jnp.float32)
    column = lax.broadcasted_iota(jnp.int32, (count, count), 1) + rank * pairs
    turn = lax.broadcasted_iota(jnp.int32, (count, count), 0) == jnp.where(column >= count, column - count, column)
    mine = jnp.dot(mine.astype(jnp.bfloat16), turn.astype(jnp.bfloat16), preferred_element_type=jnp.float32)
    chi_half = (mine + chi_ref[...]).astype(jnp.bfloat16)
    occupied = occupied_ref[:, 0:1]
    period = virtual_ref.shape[1]
    copies = []
    for index, (start, stop) in enumerate(cuts(ints_ref.shape[1], period)):
        for row in range(start, stop):
            cut = pl.ds(row * period, period)
            block = jnp.concatenate([ref[:, cut] for ref in amps], axis=0)
            ladder = jnp.dot(chi_half, block, preferred_element_type=jnp.float32).astype(jnp.bfloat16)
            total = ints_ref[:, cut].astype(jnp.float32) + ladder.astype(jnp.float32)
            buffer[:, cut] = (total / (virtual_ref[row : row + 1, :] - occupied)).astype(jnp.bfloat16)
        cut = pl.ds(start * period, (stop - start) * period)
        copy = pltpu.make_async_copy(buffer.at[:, cut], out_ref.at[:, cut], sems.at[index])
        copy.start()
        copies.append(copy)
    for copy in copies:
        copy.wait()


def team_exchange(block, team, size):
    return [
        lax.ppermute(block, "idx", [(d, (d // team) * team + (d - step) % team) for d in range(size)])
        for step in range(1, team)
    ]


def exchange_rows_16(hole):
    near, far, both = 6, 4, 2

    def by_home(d, home, away):
        at_home = (d >> 3) == (d & 1)
        if isinstance(d, int):
            return d ^ (home if at_home else away)
        return d ^ jnp.where(at_home, home, away)

    def hop_one(d):
        return by_home(d, near, far ^ 9)

    def hop_two(d):
        return by_home(d, both, both ^ 9)

    def hop_three(d):
        return d ^ 8

    def permute(block, hop):
        return lax.ppermute(block, "idx", [(d, hop(d)) for d in range(16)])

    def owners(me):
        third = hop_three(me)
        pairs = (me, hop_one(me), hop_two(me), third, hop_one(third))
        return [row for d in pairs for row in (d, d ^ 1)]

    own = jnp.concatenate([hole, permute(hole, lambda d: d ^ 1)], axis=0)
    first, second = permute(own, hop_one), permute(own, hop_two)
    forward = jnp.concatenate([own, first], axis=0)
    return [own, first, second, permute(forward, hop_three)], owners, forward


def exchange_rows(hole, team):
    sent = jnp.repeat(jnp.swapaxes(hole, 0, 1), team, axis=0)
    received = lax.all_to_all(sent, "idx", split_axis=0, concat_axis=0, tiled=True)
    return [received], lambda me: None, received


def after(block, other):
    return lax.optimization_barrier((block, other))[0]


def on_device(amplitudes, integrals, hole_integrals, occ_energy, vir_energy, pair_orbitals, size):
    local_pairs, width = amplitudes.shape
    pair_count = hole_integrals.shape[2]
    team = pair_count // local_pairs
    block = vir_energy.shape[0] // IRREPS
    period = math.lcm(block, 128)
    rows = width // period

    if size == 16 and team == 2:
        slabs, owners, last_sent = exchange_rows_16(hole_integrals)
    else:
        slabs, owners, last_sent = exchange_rows(hole_integrals, team)
    amps = [amplitudes] + team_exchange(amplitudes, team, size)
    ints = [integrals] + [after(other, last_sent) for other in team_exchange(integrals, team, size)]
    slabs = [slab.reshape(-1, pair_count) for slab in slabs]

    def near(array):
        return pltpu.with_memory_space_constraint(array, pltpu.VMEM) if team == 2 else array

    params = pltpu.CompilerParams(vmem_limit_bytes=(16 if team == 2 else 40) * 1024 * 1024)
    cost = functools.partial(pl.CostEstimate, flops=2 * local_pairs * pair_count * width, transcendentals=0)
    chi, virtual, occupied = pl.pallas_call(
        functools.partial(chi_kernel, team, rows),
        out_shape=[
            jax.ShapeDtypeStruct((local_pairs, pair_count), jnp.float32),
            jax.ShapeDtypeStruct((-(-rows // 8) * 8, period), jnp.float32),
            jax.ShapeDtypeStruct((local_pairs, 128), jnp.float32),
        ],
        in_specs=[IN_VMEM] * (4 + team),
        out_specs=[IN_VMEM] * 3,
        compiler_params=params,
        cost_estimate=cost(bytes_accessed=2 * local_pairs * width * 2),
    )(
        near(vir_energy.reshape(1, -1)),
        near(occ_energy.reshape(1, -1)),
        near(pair_orbitals.T),
        near(amplitudes),
        *[near(other) for other in ints],
    )
    return pl.pallas_call(
        functools.partial(update_kernel, team, len(slabs), owners),
        out_shape=jax.ShapeDtypeStruct((local_pairs, width), jnp.bfloat16),
        in_specs=[IN_VMEM] * (4 + len(slabs) + team),
        out_specs=pl.BlockSpec(memory_space=pl.ANY),
        scratch_shapes=[
            pltpu.VMEM((local_pairs, width), jnp.bfloat16),
            pltpu.SemaphoreType.DMA((CHUNKS,)),
        ],
        compiler_params=params,
        cost_estimate=cost(bytes_accessed=4 * local_pairs * width * 2),
    )(chi, virtual, occupied, near(integrals), *slabs, *[near(other) for other in amps])


def solution(mesh):
    size = mesh.shape["idx"]
    in_specs = (
        P(("grp", "idx"), None),
        P(("grp", "idx"), None),
        P(("grp", "idx"), None, None),
        P("grp"),
        P("grp"),
        P(("grp", "idx"), None),
    )
    out_specs = P(("grp", "idx"), None)

    def run(*args):
        return on_device(*args, size)

    return jax.shard_map(run, mesh=mesh, in_specs=in_specs, out_specs=out_specs, check_vma=False)
```

```python
import functools
import math

import jax
import jax.numpy as jnp
from jax import lax
from jax.experimental import pallas as pl
from jax.experimental.pallas import tpu as pltpu
from jax.sharding import PartitionSpec as P

IRREPS = 8
CHUNKS = 5
GROUPS = 5
IN_VMEM = pl.BlockSpec(memory_space=pltpu.VMEM)
IN_HBM = pl.BlockSpec(memory_space=pltpu.HBM)


def cuts(width, period):
    count = width // period
    edges = [count * c // CHUNKS for c in range(CHUNKS + 1)]
    return [(edge, stop) for edge, stop in zip(edges, edges[1:]) if stop > edge]


def one_hot_sum(values, columns):
    lanes = lax.broadcasted_iota(jnp.int32, (columns.shape[0], values.shape[1]), 1)
    return jnp.sum(jnp.where(lanes == columns, values, 0.0), axis=1, keepdims=True)


def occupied_sums(occ, orbitals):
    pairs = orbitals.shape[1]
    diagonal = lax.broadcasted_iota(jnp.int32, (pairs, pairs), 0) == lax.broadcasted_iota(
        jnp.int32, (pairs, pairs), 1
    )
    each = [
        one_hot_sum(occ, jnp.sum(jnp.where(diagonal, orbitals[j : j + 1, :], 0), axis=1, keepdims=True))
        for j in range(2)
    ]
    return jnp.broadcast_to(each[0] + each[1], (pairs, 128))


def virtual_sums(vir, symmetry, rows, period):
    block = vir.shape[1] // IRREPS
    step = period // block
    padded = jnp.concatenate([vir, jnp.zeros((1, 128), jnp.float32)], axis=1)
    held = -(-rows // 8) * 8
    row = lax.broadcasted_iota(jnp.int32, (held, 128), 0)
    lane = lax.broadcasted_iota(jnp.int32, (held, 128), 1)

    def irrep_of(orbital):
        return sum((orbital >= block * q).astype(jnp.int32) for q in range(1, IRREPS))

    def partner(orbital):
        other = jnp.bitwise_xor(irrep_of(orbital), symmetry)
        energies = jnp.zeros((held, 128), jnp.float32)
        for q in range(IRREPS):
            energies = jnp.where(other == q, padded[:, block * q : block * q + 128], energies)
        return energies

    firsts = [padded[:, step * r : step * r + 128] for r in range(rows)]
    first = jnp.concatenate(firsts + [jnp.zeros((held - rows, 128), jnp.float32)], axis=0)
    low, high = partner(row * step), partner(row * step + step - 1)
    turn = (irrep_of(row * step) + 1) * block
    sums = []
    for tile in range(period // 128):
        start = tile * 128 // block
        element = lane + tile * 128
        a = start + sum((element >= block * (start + q)).astype(jnp.int32) for q in range(1, 2 + 127 // block))
        b = element - a * block
        second = jnp.where(
            row * step + a >= turn, jnp.take_along_axis(high, b, axis=1), jnp.take_along_axis(low, b, axis=1)
        )
        sums.append(jnp.take_along_axis(first, a, axis=1) + second)
    return jnp.concatenate(sums, axis=1)


def chi_kernel(team, rows, vir_hbm, occ_hbm, orbitals_hbm, amps_hbm, ints_hbm, *refs):
    others = refs[: team - 1]
    chi_ref, virtual_ref, occupied_ref, amps_ref, ints_ref = refs[team - 1 : team + 4]
    vir_ref, occ_ref, orbitals_ref, sems = refs[team + 4 :]
    moves = (
        (vir_hbm, vir_ref),
        (occ_hbm, occ_ref),
        (orbitals_hbm, orbitals_ref),
        (amps_hbm, amps_ref),
        (ints_hbm, ints_ref),
    )
    copies = [pltpu.make_async_copy(*move, sems.at[slot]) for slot, move in enumerate(moves)]
    for copy in copies:
        copy.start()
    for copy in copies[:3]:
        copy.wait()
    symmetry = lax.axis_index("idx") // team
    virtual_ref[...] = virtual_sums(vir_ref[...].reshape(1, -1), symmetry, rows, virtual_ref.shape[1])
    occupied_ref[...] = occupied_sums(occ_ref[...].reshape(1, -1), orbitals_ref[...])
    for copy in copies[3:]:
        copy.wait()

    ints = (ints_ref, *others)
    pairs, width = amps_ref.shape
    part = width // GROUPS // 128 * 128
    rest = width - part * GROUPS

    def dot(spans):
        return lax.dot_general(
            jnp.concatenate([amps_ref[:, span] for span in spans], axis=0),
            jnp.concatenate([ref[:, span] for span in spans for ref in ints], axis=0),
            (((1,), (1,)), ((), ())),
            preferred_element_type=jnp.float32,
        )

    whole = dot([pl.ds(g * part, part) for g in range(GROUPS)])
    count = chi_ref.shape[1]
    total = sum(whole[g * pairs : (g + 1) * pairs, g * count : (g + 1) * count] for g in range(GROUPS))
    chi_ref[...] = total + dot([pl.ds(part * GROUPS, rest)]) if rest else total


def update_kernel(team, slabs, owners, chi_ref, virtual_ref, occupied_ref, ints_ref, *refs):
    bare, amps = refs[:slabs], refs[slabs : slabs + team]
    out_ref, buffer, sems = refs[slabs + team :]
    me = lax.axis_index("idx")
    symmetry, rank = me // team, me % team
    pairs, count = chi_ref.shape
    stack = jnp.concatenate([ref[...] for ref in bare], axis=0)
    held = owners(me)
    lane = lax.broadcasted_iota(jnp.int32, (pairs, stack.shape[0]), 1)
    if held is None:
        owner = lane
    else:
        wide = stack.shape[0] // len(held)
        owner = jnp.full(lane.shape, -1, jnp.int32)
        for slot, row in enumerate(held):
            owner = jnp.where(lane == slot * wide + symmetry, row, owner)
    pick = owner == rank * pairs + lax.broadcasted_iota(jnp.int32, lane.shape, 0)
    mine = jnp.dot(pick.astype(jnp.bfloat16), stack, preferred_element_type=jnp.float32)
    column = lax.broadcasted_iota(jnp.int32, (count, count), 1) + rank * pairs
    turn = lax.broadcasted_iota(jnp.int32, (count, count), 0) == jnp.where(column >= count, column - count, column)
    mine = jnp.dot(mine.astype(jnp.bfloat16), turn.astype(jnp.bfloat16), preferred_element_type=jnp.float32)
    chi_half = (mine + chi_ref[...]).astype(jnp.bfloat16)
    occupied = occupied_ref[:, 0:1]
    period = virtual_ref.shape[1]
    copies = []
    for index, (start, stop) in enumerate(cuts(ints_ref.shape[1], period)):
        for row in range(start, stop):
            cut = pl.ds(row * period, period)
            block = jnp.concatenate([ref[:, cut] for ref in amps], axis=0)
            ladder = jnp.dot(chi_half, block, preferred_element_type=jnp.float32).astype(jnp.bfloat16)
            total = ints_ref[:, cut].astype(jnp.float32) + ladder.astype(jnp.float32)
            buffer[:, cut] = (total / (virtual_ref[row : row + 1, :] - occupied)).astype(jnp.bfloat16)
        cut = pl.ds(start * period, (stop - start) * period)
        copy = pltpu.make_async_copy(buffer.at[:, cut], out_ref.at[:, cut], sems.at[index])
        copy.start()
        copies.append(copy)
    for copy in copies:
        copy.wait()


def team_exchange(block, team, size):
    return [
        lax.ppermute(block, "idx", [(d, (d // team) * team + (d - step) % team) for d in range(size)])
        for step in range(1, team)
    ]


def exchange_rows_16(hole):
    near, far, both = 6, 4, 2

    def by_home(d, home, away):
        at_home = (d >> 3) == (d & 1)
        if isinstance(d, int):
            return d ^ (home if at_home else away)
        return d ^ jnp.where(at_home, home, away)

    def hop_one(d):
        return by_home(d, near, far ^ 9)

    def hop_two(d):
        return by_home(d, both, both ^ 9)

    def hop_three(d):
        return d ^ 8

    def permute(block, hop):
        return lax.ppermute(block, "idx", [(d, hop(d)) for d in range(16)])

    def owners(me):
        third = hop_three(me)
        pairs = (me, hop_one(me), hop_two(me), third, hop_one(third))
        return [row for d in pairs for row in (d, d ^ 1)]

    own = jnp.concatenate([hole, permute(hole, lambda d: d ^ 1)], axis=0)
    first, second = permute(own, hop_one), permute(own, hop_two)
    forward = jnp.concatenate([own, first], axis=0)
    return [own, first, second, permute(forward, hop_three)], owners, own, forward


def exchange_rows(hole, team):
    sent = jnp.repeat(jnp.swapaxes(hole, 0, 1), team, axis=0)
    received = lax.all_to_all(sent, "idx", split_axis=0, concat_axis=0, tiled=True)
    return [received], lambda me: None, hole, received


def after(block, other):
    return lax.optimization_barrier((block, other))[0]


def on_device(amplitudes, integrals, hole_integrals, occ_energy, vir_energy, pair_orbitals, size):
    local_pairs, width = amplitudes.shape
    pair_count = hole_integrals.shape[2]
    team = pair_count // local_pairs
    block = vir_energy.shape[0] // IRREPS
    period = math.lcm(block, 128)
    rows = width // period

    def in_hbm(array):
        return pltpu.with_memory_space_constraint(array, pltpu.HBM)

    def near(array):
        return pltpu.with_memory_space_constraint(array, pltpu.VMEM) if team == 2 else array

    params = pltpu.CompilerParams(vmem_limit_bytes=(16 if team == 2 else 40) * 1024 * 1024)
    cost = functools.partial(pl.CostEstimate, flops=2 * local_pairs * pair_count * width, transcendentals=0)

    if size == 16 and team == 2:
        slabs, owners, first_sent, last_sent = exchange_rows_16(hole_integrals)
    else:
        slabs, owners, first_sent, last_sent = exchange_rows(hole_integrals, team)
    other_ints = [after(far, last_sent) for far in team_exchange(after(integrals, first_sent), team, size)]
    other_amps = team_exchange(after(amplitudes, first_sent), team, size)
    slabs = [slab.reshape(-1, pair_count) for slab in slabs]

    chi, virtual, occupied, own_amps, own_ints = pl.pallas_call(
        functools.partial(chi_kernel, team, rows),
        out_shape=[
            jax.ShapeDtypeStruct((local_pairs, pair_count), jnp.float32),
            jax.ShapeDtypeStruct((-(-rows // 8) * 8, period), jnp.float32),
            jax.ShapeDtypeStruct((local_pairs, 128), jnp.float32),
            pltpu.VMEM(amplitudes.shape, amplitudes.dtype),
            pltpu.VMEM(integrals.shape, integrals.dtype),
        ],
        in_specs=[IN_HBM] * 5 + [IN_VMEM] * (team - 1),
        out_specs=[IN_VMEM] * 5,
        scratch_shapes=[
            pltpu.VMEM(vir_energy.shape, jnp.float32),
            pltpu.VMEM(occ_energy.shape, jnp.float32),
            pltpu.VMEM((2, local_pairs), jnp.int32),
            pltpu.SemaphoreType.DMA((5,)),
        ],
        compiler_params=params,
        cost_estimate=cost(bytes_accessed=2 * amplitudes.nbytes),
    )(
        *[in_hbm(array) for array in (vir_energy, occ_energy, pair_orbitals.T, amplitudes, integrals)],
        *[near(far) for far in other_ints],
    )
    return pl.pallas_call(
        functools.partial(update_kernel, team, len(slabs), owners),
        out_shape=jax.ShapeDtypeStruct((local_pairs, width), jnp.bfloat16),
        in_specs=[IN_VMEM] * (4 + len(slabs) + team),
        out_specs=IN_HBM,
        scratch_shapes=[
            pltpu.VMEM((local_pairs, width), jnp.bfloat16),
            pltpu.SemaphoreType.DMA((CHUNKS,)),
        ],
        compiler_params=params,
        cost_estimate=cost(bytes_accessed=4 * local_pairs * width * 2),
    )(chi, virtual, occupied, own_ints, *slabs, own_amps, *[near(far) for far in other_amps])


def solution(mesh):
    size = mesh.shape["idx"]
    in_specs = (
        P(("grp", "idx"), None),
        P(("grp", "idx"), None),
        P(("grp", "idx"), None, None),
        P("grp"),
        P("grp"),
        P(("grp", "idx"), None),
    )
    out_specs = P(("grp", "idx"), None)

    def run(*args):
        return on_device(*args, size)

    return jax.shard_map(run, mesh=mesh, in_specs=in_specs, out_specs=out_specs, check_vma=False)
```

```python
import functools
import itertools
import math

import jax
import jax.numpy as jnp
from jax import lax
from jax.experimental import pallas as pl
from jax.experimental.pallas import tpu as pltpu
from jax.sharding import PartitionSpec as P

IRREPS = 8
GROUPS = 5
IN_VMEM = pl.BlockSpec(memory_space=pltpu.VMEM)
IN_HBM = pl.BlockSpec(memory_space=pltpu.HBM)


def one_hot_sum(values, columns):
    lanes = lax.broadcasted_iota(jnp.int32, (columns.shape[0], values.shape[1]), 1)
    return jnp.sum(jnp.where(lanes == columns, values, 0.0), axis=1, keepdims=True)


def occupied_sums(occ, orbitals):
    pairs = orbitals.shape[1]
    diagonal = lax.broadcasted_iota(jnp.int32, (pairs, pairs), 0) == lax.broadcasted_iota(
        jnp.int32, (pairs, pairs), 1
    )
    each = [
        one_hot_sum(occ, jnp.sum(jnp.where(diagonal, orbitals[j : j + 1, :], 0), axis=1, keepdims=True))
        for j in range(2)
    ]
    return jnp.broadcast_to(each[0] + each[1], (pairs, 128))


def irrep_tiles(block):
    return [g * block * block // 128 for g in range(IRREPS)] + [-(-IRREPS * block * block // 128)]


def virtual_sums(vir, symmetry, tiles):
    block = vir.shape[1] // IRREPS
    padded = jnp.concatenate([vir, jnp.zeros((1, 128), jnp.float32)], axis=1)
    energies = [padded[:, block * g : block * g + 128] for g in range(IRREPS)]
    first = jnp.concatenate(energies, axis=0)
    row = lax.broadcasted_iota(jnp.int32, (IRREPS, 128), 0)
    lane = lax.broadcasted_iota(jnp.int32, (IRREPS, 128), 1)
    other = jnp.bitwise_xor(row, symmetry)
    second = jnp.zeros((IRREPS, 128), jnp.float32)
    for g in range(IRREPS):
        second = jnp.where(other == g, energies[g], second)
    lead = (row * (block * block)) % 128
    sums = []
    for tile in range(tiles):
        element = jnp.clip(lane + tile * 128 - lead, 0, block * block - 1)
        least = max(0, tile * 128 - 127) // block
        a = least + sum((element >= block * (least + q)).astype(jnp.int32) for q in range(1, 3 + 254 // block))
        b = element - a * block
        sums.append(jnp.take_along_axis(first, a, axis=1) + jnp.take_along_axis(second, b, axis=1))
    starts = irrep_tiles(block)
    ends = jnp.zeros((IRREPS, 128), jnp.float32)
    for g in range(1, IRREPS):
        ends = jnp.where(row == g, sums[starts[g] - starts[g - 1]][g - 1 : g, :], ends)
    sums[0] = jnp.where(lane < lead, ends, sums[0])
    return jnp.concatenate(sums, axis=1)


def load_kernel(team, vir_hbm, occ_hbm, orbitals_hbm, hole_hbm, amps_hbm, ints_hbm, *refs):
    virtual_ref, occupied_ref, hole_ref, tiles_ref, vir_ref, occ_ref, orbitals_ref, sems = refs
    moves = (
        (vir_hbm, vir_ref),
        (occ_hbm, occ_ref),
        (orbitals_hbm, orbitals_ref),
        (hole_hbm, hole_ref),
        (amps_hbm, tiles_ref.at[0]),
        (ints_hbm, tiles_ref.at[1]),
    )
    copies = [pltpu.make_async_copy(*move, sems.at[slot]) for slot, move in enumerate(moves)]
    for copy in copies:
        copy.start()
    for copy in copies[:3]:
        copy.wait()
    symmetry = lax.axis_index("idx") // team
    virtual_ref[...] = virtual_sums(vir_ref[...].reshape(1, -1), symmetry, virtual_ref.shape[1] // 128)
    occupied_ref[...] = occupied_sums(occ_ref[...].reshape(1, -1), orbitals_ref[...])
    for copy in copies[3:]:
        copy.wait()


def folded_dot(left, rights):
    pairs, width = left.shape
    part = width // GROUPS // 128 * 128
    rest = width - part * GROUPS
    count = sum(ref.shape[0] for ref in rights)

    def dot(spans):
        return lax.dot_general(
            jnp.concatenate([left[:, span] for span in spans], axis=0),
            jnp.concatenate([ref[:, span] for span in spans for ref in rights], axis=0),
            (((1,), (1,)), ((), ())),
            preferred_element_type=jnp.float32,
        )

    whole = dot([pl.ds(g * part, part) for g in range(GROUPS)])
    total = sum(whole[g * pairs : (g + 1) * pairs, g * count : (g + 1) * count] for g in range(GROUPS))
    return total + dot([pl.ds(part * GROUPS, rest)]) if rest else total


def chi_kernel(*refs):
    tiles, chi_ref = refs[:-1], refs[-1]
    chi_ref[...] = folded_dot(tiles[0].at[0], [ref.at[1] for ref in tiles])


def update_kernel(team, slabs, owners, chi_ref, virtual_ref, occupied_ref, *refs):
    bare, tiles = refs[:slabs], refs[slabs : slabs + team]
    ints_ref, amps = tiles[0].at[1], [ref.at[0] for ref in tiles]
    out_ref, buffer, sems = refs[slabs + team :]
    me = lax.axis_index("idx")
    symmetry, rank = me // team, me % team
    pairs, count = chi_ref.shape
    stack = jnp.concatenate([ref[...] for ref in bare], axis=0)
    held = owners(me)
    lane = lax.broadcasted_iota(jnp.int32, (pairs, stack.shape[0]), 1)
    if held is None:
        owner = lane
    else:
        wide = stack.shape[0] // len(held)
        owner = jnp.full(lane.shape, -1, jnp.int32)
        for slot, row in enumerate(held):
            owner = jnp.where(lane == slot * wide + symmetry, row, owner)
    pick = owner == rank * pairs + lax.broadcasted_iota(jnp.int32, lane.shape, 0)
    mine = jnp.dot(pick.astype(jnp.bfloat16), stack, preferred_element_type=jnp.float32)
    column = lax.broadcasted_iota(jnp.int32, (count, count), 1) + rank * pairs
    turn = lax.broadcasted_iota(jnp.int32, (count, count), 0) == jnp.where(column >= count, column - count, column)
    mine = jnp.dot(mine.astype(jnp.bfloat16), turn.astype(jnp.bfloat16), preferred_element_type=jnp.float32)
    chi_half = (mine + chi_ref[...]).astype(jnp.bfloat16)
    occupied = occupied_ref[:, 0:1]
    width = ints_ref.shape[1]
    copies = []
    for g, (start, end) in enumerate(itertools.pairwise(irrep_tiles(math.isqrt(width // IRREPS)))):
        cut = pl.ds(start * 128, (end - start) * 128)
        block = jnp.concatenate([ref[:, cut] for ref in amps], axis=0)
        ladder = jnp.dot(chi_half, block, preferred_element_type=jnp.float32).astype(jnp.bfloat16)
        total = ints_ref[:, cut].astype(jnp.float32) + ladder.astype(jnp.float32)
        denominator = virtual_ref[g : g + 1, : (end - start) * 128] - occupied
        buffer[:, cut] = (total / denominator).astype(jnp.bfloat16)
        copy = pltpu.make_async_copy(buffer.at[:, cut], out_ref.at[:, cut], sems.at[g])
        copy.start()
        copies.append(copy)
    for copy in copies:
        copy.wait()


def team_exchange(block, team, size):
    return [
        lax.ppermute(block, "idx", [(d, (d // team) * team + (d - step) % team) for d in range(size)])
        for step in range(1, team)
    ]


def exchange_rows_16(hole, near_hole):
    near, far, both = 6, 4, 2

    def by_home(d, home, away):
        at_home = (d >> 3) == (d & 1)
        if isinstance(d, int):
            return d ^ (home if at_home else away)
        return d ^ jnp.where(at_home, home, away)

    def hop_one(d):
        return by_home(d, near, far ^ 9)

    def hop_two(d):
        return by_home(d, both, both ^ 9)

    def hop_three(d):
        return d ^ 8

    def permute(block, hop):
        return lax.ppermute(block, "idx", [(d, hop(d)) for d in range(16)])

    def owners(me):
        third = hop_three(me)
        pairs = (me, hop_one(me), hop_two(me), third, hop_one(third))
        return [row for d in pairs for row in (d, d ^ 1)]

    own = jnp.concatenate([near_hole, permute(hole, lambda d: d ^ 1)], axis=0)
    first, second = permute(own, hop_one), permute(own, hop_two)
    forward = jnp.concatenate([own, first], axis=0)
    return [own, first, second, permute(forward, hop_three)], owners, own, forward


def exchange_rows(hole, team):
    sent = jnp.repeat(jnp.swapaxes(hole, 0, 1), team, axis=0)
    received = lax.all_to_all(sent, "idx", split_axis=0, concat_axis=0, tiled=True)
    return [received], lambda me: None, hole, received


def after(block, other):
    return lax.optimization_barrier((block, other))[0]


def on_device(amplitudes, integrals, hole_integrals, occ_energy, vir_energy, pair_orbitals, size):
    local_pairs, width = amplitudes.shape
    pair_count = hole_integrals.shape[2]
    team = pair_count // local_pairs
    block = vir_energy.shape[0] // IRREPS
    tiles = max(end - start for start, end in itertools.pairwise(irrep_tiles(block))) + 1

    def in_hbm(array):
        return pltpu.with_memory_space_constraint(array, pltpu.HBM)

    def near(array):
        return pltpu.with_memory_space_constraint(array, pltpu.VMEM) if team == 2 else array

    params = pltpu.CompilerParams(vmem_limit_bytes=(16 if team == 2 else 40) * 1024 * 1024)
    cost = functools.partial(pl.CostEstimate, flops=2 * local_pairs * pair_count * width, transcendentals=0)

    virtual, occupied, near_hole, own = pl.pallas_call(
        functools.partial(load_kernel, team),
        out_shape=[
            jax.ShapeDtypeStruct((IRREPS, tiles * 128), jnp.float32),
            jax.ShapeDtypeStruct((local_pairs, 128), jnp.float32),
            pltpu.VMEM(hole_integrals.shape, hole_integrals.dtype),
            pltpu.VMEM((2, *amplitudes.shape), amplitudes.dtype),
        ],
        in_specs=[IN_HBM] * 6,
        out_specs=[IN_VMEM] * 4,
        scratch_shapes=[
            pltpu.VMEM(vir_energy.shape, jnp.float32),
            pltpu.VMEM(occ_energy.shape, jnp.float32),
            pltpu.VMEM((2, local_pairs), jnp.int32),
            pltpu.SemaphoreType.DMA((6,)),
        ],
        compiler_params=params,
        cost_estimate=pl.CostEstimate(flops=0, bytes_accessed=2 * amplitudes.nbytes, transcendentals=0),
    )(
        *[in_hbm(array) for array in (vir_energy, occ_energy, pair_orbitals.T)],
        *[in_hbm(array) for array in (hole_integrals, amplitudes, integrals)],
    )

    if size == 16 and team == 2:
        slabs, owners, first_sent, last_sent = exchange_rows_16(hole_integrals, near_hole)
    else:
        slabs, owners, first_sent, last_sent = exchange_rows(hole_integrals, team)
    others = [after(far, last_sent) for far in team_exchange(after(own, first_sent), team, size)]
    held = [near(tile) for tile in (own, *others)]
    slabs = [slab.reshape(-1, pair_count) for slab in slabs]

    chi = pl.pallas_call(
        chi_kernel,
        out_shape=jax.ShapeDtypeStruct((local_pairs, pair_count), jnp.float32),
        in_specs=[IN_VMEM] * team,
        out_specs=IN_VMEM,
        compiler_params=params,
        cost_estimate=cost(bytes_accessed=2 * amplitudes.nbytes),
    )(*held)
    return pl.pallas_call(
        functools.partial(update_kernel, team, len(slabs), owners),
        out_shape=jax.ShapeDtypeStruct((local_pairs, width), jnp.bfloat16),
        in_specs=[IN_VMEM] * (3 + len(slabs) + team),
        out_specs=IN_HBM,
        scratch_shapes=[
            pltpu.VMEM((local_pairs, width), jnp.bfloat16),
            pltpu.SemaphoreType.DMA((IRREPS,)),
        ],
        compiler_params=params,
        cost_estimate=cost(bytes_accessed=4 * local_pairs * width * 2),
    )(chi, virtual, occupied, *slabs, *held)


def solution(mesh):
    size = mesh.shape["idx"]
    in_specs = (
        P(("grp", "idx"), None),
        P(("grp", "idx"), None),
        P(("grp", "idx"), None, None),
        P("grp"),
        P("grp"),
        P(("grp", "idx"), None),
    )
    out_specs = P(("grp", "idx"), None)

    def run(*args):
        return on_device(*args, size)

    return jax.shard_map(run, mesh=mesh, in_specs=in_specs, out_specs=out_specs, check_vma=False)
```

```python
import functools
import itertools
import math

import jax
import jax.numpy as jnp
from jax import lax
from jax.experimental import pallas as pl
from jax.experimental.pallas import tpu as pltpu
from jax.sharding import PartitionSpec as P

IRREPS = 8
GROUPS = 5
IN_VMEM = pl.BlockSpec(memory_space=pltpu.VMEM)
IN_HBM = pl.BlockSpec(memory_space=pltpu.HBM)


def one_hot_sum(values, columns):
    lanes = lax.broadcasted_iota(jnp.int32, (columns.shape[0], values.shape[1]), 1)
    return jnp.sum(jnp.where(lanes == columns, values, 0.0), axis=1, keepdims=True)


def occupied_sums(occ, orbitals):
    pairs = orbitals.shape[1]
    diagonal = lax.broadcasted_iota(jnp.int32, (pairs, pairs), 0) == lax.broadcasted_iota(
        jnp.int32, (pairs, pairs), 1
    )
    each = [
        one_hot_sum(occ, jnp.sum(jnp.where(diagonal, orbitals[j : j + 1, :], 0), axis=1, keepdims=True))
        for j in range(2)
    ]
    return jnp.broadcast_to(each[0] + each[1], (pairs, 128))


def irrep_tiles(block):
    return [g * block * block // 128 for g in range(IRREPS)] + [-(-IRREPS * block * block // 128)]


def virtual_sums(vir, symmetry, tiles):
    block = vir.shape[1] // IRREPS
    padded = jnp.concatenate([vir, jnp.zeros((1, 128), jnp.float32)], axis=1)
    energies = [padded[:, block * g : block * g + 128] for g in range(IRREPS)]
    first = jnp.concatenate(energies, axis=0)
    row = lax.broadcasted_iota(jnp.int32, (IRREPS, 128), 0)
    lane = lax.broadcasted_iota(jnp.int32, (IRREPS, 128), 1)
    other = jnp.bitwise_xor(row, symmetry)
    second = jnp.zeros((IRREPS, 128), jnp.float32)
    for g in range(IRREPS):
        second = jnp.where(other == g, energies[g], second)
    lead = (row * (block * block)) % 128
    sums = []
    for tile in range(tiles):
        element = jnp.clip(lane + tile * 128 - lead, 0, block * block - 1)
        least = max(0, tile * 128 - 127) // block
        a = least + sum((element >= block * (least + q)).astype(jnp.int32) for q in range(1, 3 + 254 // block))
        b = element - a * block
        sums.append(jnp.take_along_axis(first, a, axis=1) + jnp.take_along_axis(second, b, axis=1))
    starts = irrep_tiles(block)
    ends = jnp.zeros((IRREPS, 128), jnp.float32)
    for g in range(1, IRREPS):
        ends = jnp.where(row == g, sums[starts[g] - starts[g - 1]][g - 1 : g, :], ends)
    sums[0] = jnp.where(lane < lead, ends, sums[0])
    return jnp.concatenate(sums, axis=1)


def load_kernel(team, vir_hbm, occ_hbm, orbitals_hbm, hole_hbm, amps_hbm, ints_hbm, *refs):
    virtual_ref, occupied_ref, hole_ref, tiles_ref, vir_ref, occ_ref, orbitals_ref, sems = refs
    moves = (
        (vir_hbm, vir_ref),
        (occ_hbm, occ_ref),
        (orbitals_hbm, orbitals_ref),
        (hole_hbm, hole_ref),
        (amps_hbm, tiles_ref.at[0]),
        (ints_hbm, tiles_ref.at[1]),
    )
    copies = [pltpu.make_async_copy(*move, sems.at[slot]) for slot, move in enumerate(moves)]
    for copy in copies:
        copy.start()
    for copy in copies[:3]:
        copy.wait()
    symmetry = lax.axis_index("idx") // team
    virtual_ref[...] = virtual_sums(vir_ref[...].reshape(1, -1), symmetry, virtual_ref.shape[1] // 128)
    occupied_ref[...] = occupied_sums(occ_ref[...].reshape(1, -1), orbitals_ref[...])
    for copy in copies[3:]:
        copy.wait()


def folded_dot(left, rights):
    pairs, width = left.shape
    part = width // GROUPS // 128 * 128
    rest = width - part * GROUPS
    count = sum(ref.shape[0] for ref in rights)

    def dot(spans):
        return lax.dot_general(
            jnp.concatenate([left[:, span] for span in spans], axis=0),
            jnp.concatenate([ref[:, span] for span in spans for ref in rights], axis=0),
            (((1,), (1,)), ((), ())),
            preferred_element_type=jnp.float32,
        )

    whole = dot([pl.ds(g * part, part) for g in range(GROUPS)])
    total = sum(whole[g * pairs : (g + 1) * pairs, g * count : (g + 1) * count] for g in range(GROUPS))
    return total + dot([pl.ds(part * GROUPS, rest)]) if rest else total


def bare_rows(team, pairs, stack, held, me):
    symmetry, rank = me // team, me % team
    lane = lax.broadcasted_iota(jnp.int32, (pairs, stack.shape[0]), 1)
    owner = lane
    if held is not None:
        wide = stack.shape[0] // len(held)
        owner = jnp.full(lane.shape, -1, jnp.int32)
        for slot, row in enumerate(held):
            owner = jnp.where(lane == slot * wide + symmetry, row, owner)
    pick = owner == rank * pairs + lax.broadcasted_iota(jnp.int32, lane.shape, 0)
    rows = jnp.dot(pick.astype(jnp.bfloat16), stack, preferred_element_type=jnp.float32)
    if held is None:
        return rows
    turned = rows
    for other in range(1, team):
        cut = other * pairs
        turned = jnp.where(rank == other, jnp.concatenate([rows[:, cut:], rows[:, :cut]], axis=1), turned)
    return turned


def chi_kernel(team, slabs, owners, *refs):
    bare, tiles, chi_ref = refs[:slabs], refs[slabs:-1], refs[-1]
    chi = folded_dot(tiles[0].at[0], [ref.at[1] for ref in tiles])
    if bare:
        me = lax.axis_index("idx")
        stack = jnp.concatenate([ref[...] for ref in bare], axis=0)
        chi += bare_rows(team, chi_ref.shape[0], stack, owners(me)[0], me)
    chi_ref[...] = chi


def update_kernel(team, slabs, owners, chi_ref, virtual_ref, occupied_ref, *refs):
    bare, tiles = refs[:slabs], refs[slabs : slabs + team]
    ints_ref, amps = tiles[0].at[1], [ref.at[0] for ref in tiles]
    out_ref, buffer, sems = refs[slabs + team :]
    me = lax.axis_index("idx")
    stack = jnp.concatenate([ref[...] for ref in bare], axis=0)
    mine = bare_rows(team, chi_ref.shape[0], stack, owners(me)[1], me)
    chi_half = (mine + chi_ref[...]).astype(jnp.bfloat16)
    occupied = occupied_ref[:, 0:1]
    width = ints_ref.shape[1]
    copies = []
    for g, (start, end) in enumerate(itertools.pairwise(irrep_tiles(math.isqrt(width // IRREPS)))):
        cut = pl.ds(start * 128, (end - start) * 128)
        block = jnp.concatenate([ref[:, cut] for ref in amps], axis=0)
        ladder = jnp.dot(chi_half, block, preferred_element_type=jnp.float32).astype(jnp.bfloat16)
        total = ints_ref[:, cut].astype(jnp.float32) + ladder.astype(jnp.float32)
        denominator = virtual_ref[g : g + 1, : (end - start) * 128] - occupied
        buffer[:, cut] = (total / denominator).astype(jnp.bfloat16)
        copy = pltpu.make_async_copy(buffer.at[:, cut], out_ref.at[:, cut], sems.at[g])
        copy.start()
        copies.append(copy)
    for copy in copies:
        copy.wait()


def team_exchange(block, team, size):
    return [
        lax.ppermute(block, "idx", [(d, (d // team) * team + (d - step) % team) for d in range(size)])
        for step in range(1, team)
    ]


def exchange_rows_16(hole, near_hole):
    def by_home(d, home, away):
        at_home = (d >> 3) == (d & 1)
        if isinstance(d, int):
            return d ^ (home if at_home else away)
        return d ^ jnp.where(at_home, home, away)

    def hop_one(d):
        return by_home(d, 6, 13)

    def hop_two(d):
        return by_home(d, 4, 11)

    def hop_three(d):
        return by_home(d, 8, 3)

    def from_three(d):
        return by_home(d, 3, 8)

    def permute(block, hop):
        return lax.ppermute(block, "idx", [(d, hop(d)) for d in range(16)])

    def owners(me):
        third = from_three(me)
        early, last = (me, hop_one(me)), (hop_two(me), third, hop_one(third))
        return [[row for d in pairs for row in (d, d ^ 1)] for pairs in (early, last)]

    own = jnp.concatenate([near_hole, permute(hole, lambda d: d ^ 1)], axis=0)
    first, second = permute(own, hop_one), permute(own, hop_two)
    forward = jnp.concatenate([own, first], axis=0)
    return [own, first], [second, permute(forward, hop_three)], owners, own, forward


def exchange_rows(hole, team):
    share = hole.shape[2] // team
    sent = jnp.stack([jnp.roll(hole, -rank * share, axis=2) for rank in range(team)], axis=2)
    sent = jnp.moveaxis(sent, 0, 2).reshape(IRREPS * team, *hole.shape[::2])
    received = lax.all_to_all(sent, "idx", split_axis=0, concat_axis=0, tiled=True)
    return [], [received], lambda me: (None, None), hole, received


def after(block, other):
    return lax.optimization_barrier((block, other))[0]


def on_device(amplitudes, integrals, hole_integrals, occ_energy, vir_energy, pair_orbitals, size):
    local_pairs, width = amplitudes.shape
    pair_count = hole_integrals.shape[2]
    team = pair_count // local_pairs
    block = vir_energy.shape[0] // IRREPS
    tiles = max(end - start for start, end in itertools.pairwise(irrep_tiles(block))) + 1

    def in_hbm(array):
        return pltpu.with_memory_space_constraint(array, pltpu.HBM)

    def near(array):
        return pltpu.with_memory_space_constraint(array, pltpu.VMEM) if team == 2 else array

    params = pltpu.CompilerParams(vmem_limit_bytes=(16 if team == 2 else 40) * 1024 * 1024)
    cost = functools.partial(pl.CostEstimate, flops=2 * local_pairs * pair_count * width, transcendentals=0)

    virtual, occupied, near_hole, own = pl.pallas_call(
        functools.partial(load_kernel, team),
        out_shape=[
            jax.ShapeDtypeStruct((IRREPS, tiles * 128), jnp.float32),
            jax.ShapeDtypeStruct((local_pairs, 128), jnp.float32),
            pltpu.VMEM(hole_integrals.shape, hole_integrals.dtype),
            pltpu.VMEM((2, *amplitudes.shape), amplitudes.dtype),
        ],
        in_specs=[IN_HBM] * 6,
        out_specs=[IN_VMEM] * 4,
        scratch_shapes=[
            pltpu.VMEM(vir_energy.shape, jnp.float32),
            pltpu.VMEM(occ_energy.shape, jnp.float32),
            pltpu.VMEM((2, local_pairs), jnp.int32),
            pltpu.SemaphoreType.DMA((6,)),
        ],
        compiler_params=params,
        cost_estimate=pl.CostEstimate(flops=0, bytes_accessed=2 * amplitudes.nbytes, transcendentals=0),
    )(
        *[in_hbm(array) for array in (vir_energy, occ_energy, pair_orbitals.T)],
        *[in_hbm(array) for array in (hole_integrals, amplitudes, integrals)],
    )

    if size == 16 and team == 2:
        early, late, owners, first_sent, last_sent = exchange_rows_16(hole_integrals, near_hole)
    else:
        early, late, owners, first_sent, last_sent = exchange_rows(hole_integrals, team)
    others = [after(far, last_sent) for far in team_exchange(after(own, first_sent), team, size)]
    held = [near(tile) for tile in (own, *others)]
    early, late = [[slab.reshape(-1, pair_count) for slab in slabs] for slabs in (early, late)]

    chi = pl.pallas_call(
        functools.partial(chi_kernel, team, len(early), owners),
        out_shape=jax.ShapeDtypeStruct((local_pairs, pair_count), jnp.float32),
        in_specs=[IN_VMEM] * (len(early) + team),
        out_specs=IN_VMEM,
        compiler_params=params,
        cost_estimate=cost(bytes_accessed=2 * amplitudes.nbytes),
    )(*early, *held)
    return pl.pallas_call(
        functools.partial(update_kernel, team, len(late), owners),
        out_shape=jax.ShapeDtypeStruct((local_pairs, width), jnp.bfloat16),
        in_specs=[IN_VMEM] * (3 + len(late) + team),
        out_specs=IN_HBM,
        scratch_shapes=[
            pltpu.VMEM((local_pairs, width), jnp.bfloat16),
            pltpu.SemaphoreType.DMA((IRREPS,)),
        ],
        compiler_params=params,
        cost_estimate=cost(bytes_accessed=4 * local_pairs * width * 2),
    )(chi, virtual, occupied, *late, *held)


def solution(mesh):
    size = mesh.shape["idx"]
    in_specs = (
        P(("grp", "idx"), None),
        P(("grp", "idx"), None),
        P(("grp", "idx"), None, None),
        P("grp"),
        P("grp"),
        P(("grp", "idx"), None),
    )
    out_specs = P(("grp", "idx"), None)

    def run(*args):
        return on_device(*args, size)

    return jax.shard_map(run, mesh=mesh, in_specs=in_specs, out_specs=out_specs, check_vma=False)
```

```python
import functools
import itertools
import math

import jax
import jax.numpy as jnp
from jax import lax
from jax.experimental import pallas as pl
from jax.experimental.pallas import tpu as pltpu
from jax.sharding import PartitionSpec as P

IRREPS = 8
GROUPS = 5
IN_VMEM = pl.BlockSpec(memory_space=pltpu.VMEM)
IN_HBM = pl.BlockSpec(memory_space=pltpu.HBM)


def one_hot_sum(values, columns):
    lanes = lax.broadcasted_iota(jnp.int32, (columns.shape[0], values.shape[1]), 1)
    return jnp.sum(jnp.where(lanes == columns, values, 0.0), axis=1, keepdims=True)


def occupied_sums(occ, orbitals):
    pairs = orbitals.shape[1]
    diagonal = lax.broadcasted_iota(jnp.int32, (pairs, pairs), 0) == lax.broadcasted_iota(
        jnp.int32, (pairs, pairs), 1
    )
    each = [
        one_hot_sum(occ, jnp.sum(jnp.where(diagonal, orbitals[j : j + 1, :], 0), axis=1, keepdims=True))
        for j in range(2)
    ]
    return jnp.broadcast_to(each[0] + each[1], (pairs, 128))


def irrep_tiles(block):
    return [g * block * block // 128 for g in range(IRREPS)] + [-(-IRREPS * block * block // 128)]


def virtual_sums(vir, symmetry, tiles):
    block = vir.shape[1] // IRREPS
    padded = jnp.concatenate([vir, jnp.zeros((1, 128), jnp.float32)], axis=1)
    energies = [padded[:, block * g : block * g + 128] for g in range(IRREPS)]
    first = jnp.concatenate(energies, axis=0)
    row = lax.broadcasted_iota(jnp.int32, (IRREPS, 128), 0)
    lane = lax.broadcasted_iota(jnp.int32, (IRREPS, 128), 1)
    other = jnp.bitwise_xor(row, symmetry)
    second = jnp.zeros((IRREPS, 128), jnp.float32)
    for g in range(IRREPS):
        second = jnp.where(other == g, energies[g], second)
    lead = (row * (block * block)) % 128
    sums = []
    for tile in range(tiles):
        element = jnp.clip(lane + tile * 128 - lead, 0, block * block - 1)
        least = max(0, tile * 128 - 127) // block
        a = least + sum((element >= block * (least + q)).astype(jnp.int32) for q in range(1, 3 + 254 // block))
        b = element - a * block
        sums.append(jnp.take_along_axis(first, a, axis=1) + jnp.take_along_axis(second, b, axis=1))
    starts = irrep_tiles(block)
    ends = jnp.zeros((IRREPS, 128), jnp.float32)
    for g in range(1, IRREPS):
        ends = jnp.where(row == g, sums[starts[g] - starts[g - 1]][g - 1 : g, :], ends)
    sums[0] = jnp.where(lane < lead, ends, sums[0])
    return jnp.concatenate(sums, axis=1)


def tile_copies(amps_hbm, ints_hbm, tiles_ref, sems):
    return [
        pltpu.make_async_copy(source, tiles_ref.at[which], sems.at[which])
        for which, source in enumerate((amps_hbm, ints_hbm))
    ]


def load_kernel(here, *refs):
    small, (amps_hbm, ints_hbm), targets = refs[:4], refs[4:6], refs[6:10]
    tiles_ref, sems, tile_sems = refs[10:]
    copies = [pltpu.make_async_copy(*move, sems.at[slot]) for slot, move in enumerate(zip(small, targets))]
    for copy in copies:
        copy.start()

    @pl.when(lax.axis_index("idx") < here)
    def _():
        tiles = tile_copies(amps_hbm, ints_hbm, tiles_ref, tile_sems)
        for copy in tiles:
            copy.start()
        for copy in tiles:
            copy.wait()

    for copy in copies:
        copy.wait()


def folded_dot(left, rights):
    pairs, width = left.shape
    part = width // GROUPS // 128 * 128
    rest = width - part * GROUPS
    count = sum(ref.shape[0] for ref in rights)

    def dot(spans):
        return lax.dot_general(
            jnp.concatenate([left[:, span] for span in spans], axis=0),
            jnp.concatenate([ref[:, span] for span in spans for ref in rights], axis=0),
            (((1,), (1,)), ((), ())),
            preferred_element_type=jnp.float32,
        )

    whole = dot([pl.ds(g * part, part) for g in range(GROUPS)])
    total = sum(whole[g * pairs : (g + 1) * pairs, g * count : (g + 1) * count] for g in range(GROUPS))
    return total + dot([pl.ds(part * GROUPS, rest)]) if rest else total


def bare_rows(team, pairs, stack, held, me):
    symmetry, rank = me // team, me % team
    lane = lax.broadcasted_iota(jnp.int32, (pairs, stack.shape[0]), 1)
    owner = lane
    if held is not None:
        wide = stack.shape[0] // len(held)
        owner = jnp.full(lane.shape, -1, jnp.int32)
        for slot, row in enumerate(held):
            owner = jnp.where(lane == slot * wide + symmetry, row, owner)
    pick = owner == rank * pairs + lax.broadcasted_iota(jnp.int32, lane.shape, 0)
    rows = jnp.dot(pick.astype(jnp.bfloat16), stack, preferred_element_type=jnp.float32)
    if held is None:
        return rows
    turned = rows
    for other in range(1, team):
        cut = other * pairs
        turned = jnp.where(rank == other, jnp.concatenate([rows[:, cut:], rows[:, :cut]], axis=1), turned)
    return turned


def chi_kernel(team, here, slabs, owners, amps_hbm, ints_hbm, held_ref, vir_ref, occ_ref, orbitals_ref, *refs):
    bare, ints = refs[:slabs], refs[slabs : slabs + team - 1]
    chi_ref, tiles_ref, virtual_ref, occupied_ref, sems = refs[slabs + team - 1 :]
    me = lax.axis_index("idx")

    @pl.when(me >= here)
    def _():
        copies = tile_copies(amps_hbm, ints_hbm, tiles_ref, sems)
        for copy in copies:
            copy.start()
        for copy in copies:
            copy.wait()

    virtual_ref[...] = virtual_sums(vir_ref[...].reshape(1, -1), me // team, virtual_ref.shape[1] // 128)
    occupied_ref[...] = occupied_sums(occ_ref[...].reshape(1, -1), orbitals_ref[...])
    chi = folded_dot(tiles_ref.at[0], [tiles_ref.at[1], *ints])
    if bare:
        stack = jnp.concatenate([ref[...] for ref in bare], axis=0)
        chi += bare_rows(team, chi_ref.shape[0], stack, owners(me)[0], me)
    chi_ref[...] = chi


def update_kernel(team, slabs, owners, chi_ref, virtual_ref, occupied_ref, *refs):
    bare, tiles_ref = refs[:slabs], refs[slabs]
    ints_ref, amps = tiles_ref.at[1], [tiles_ref.at[0], *refs[slabs + 1 : slabs + team]]
    out_ref, buffer, sems = refs[slabs + team :]
    me = lax.axis_index("idx")
    stack = jnp.concatenate([ref[...] for ref in bare], axis=0)
    mine = bare_rows(team, chi_ref.shape[0], stack, owners(me)[1], me)
    chi_half = (mine + chi_ref[...]).astype(jnp.bfloat16)
    occupied = occupied_ref[:, 0:1]
    width = ints_ref.shape[1]
    copies = []
    for g, (start, end) in enumerate(itertools.pairwise(irrep_tiles(math.isqrt(width // IRREPS)))):
        cut = pl.ds(start * 128, (end - start) * 128)
        block = jnp.concatenate([ref[:, cut] for ref in amps], axis=0)
        ladder = jnp.dot(chi_half, block, preferred_element_type=jnp.float32).astype(jnp.bfloat16)
        total = ints_ref[:, cut].astype(jnp.float32) + ladder.astype(jnp.float32)
        denominator = virtual_ref[g : g + 1, : (end - start) * 128] - occupied
        buffer[:, cut] = (total / denominator).astype(jnp.bfloat16)
        copy = pltpu.make_async_copy(buffer.at[:, cut], out_ref.at[:, cut], sems.at[g])
        copy.start()
        copies.append(copy)
    for copy in copies:
        copy.wait()


def team_exchange(block, team, size):
    return [
        lax.ppermute(block, "idx", [(d, (d // team) * team + (d - step) % team) for d in range(size)])
        for step in range(1, team)
    ]


def exchange_rows_16(hole, near_hole):
    def by_home(d, home, away):
        at_home = (d >> 3) == (d & 1)
        if isinstance(d, int):
            return d ^ (home if at_home else away)
        return d ^ jnp.where(at_home, home, away)

    def hop_one(d):
        return by_home(d, 6, 13)

    def hop_two(d):
        return by_home(d, 4, 11)

    def hop_three(d):
        return by_home(d, 8, 3)

    def from_three(d):
        return by_home(d, 3, 8)

    def permute(block, hop):
        return lax.ppermute(block, "idx", [(d, hop(d)) for d in range(16)])

    def owners(me):
        third = from_three(me)
        early, last = (me, hop_one(me)), (hop_two(me), third, hop_one(third))
        return [[row for d in pairs for row in (d, d ^ 1)] for pairs in (early, last)]

    own = jnp.concatenate([near_hole, permute(hole, lambda d: d ^ 1)], axis=0)
    first, second = permute(own, hop_one), permute(own, hop_two)
    forward = jnp.concatenate([own, first], axis=0)
    return [own, first], [second, permute(forward, hop_three)], owners, own, forward


def exchange_rows(hole, team):
    share = hole.shape[2] // team
    sent = jnp.stack([jnp.roll(hole, -rank * share, axis=2) for rank in range(team)], axis=2)
    sent = jnp.moveaxis(sent, 0, 2).reshape(IRREPS * team, *hole.shape[::2])
    received = lax.all_to_all(sent, "idx", split_axis=0, concat_axis=0, tiled=True)
    return [], [received], lambda me: (None, None), hole, received


def after(block, other):
    return lax.optimization_barrier((block, other))[0]


def on_device(amplitudes, integrals, hole_integrals, occ_energy, vir_energy, pair_orbitals, size):
    local_pairs, width = amplitudes.shape
    pair_count = hole_integrals.shape[2]
    team = pair_count // local_pairs
    block = vir_energy.shape[0] // IRREPS
    tiles = max(end - start for start, end in itertools.pairwise(irrep_tiles(block))) + 1

    def in_hbm(array):
        return pltpu.with_memory_space_constraint(array, pltpu.HBM)

    def near(array):
        return pltpu.with_memory_space_constraint(array, pltpu.VMEM) if team == 2 else array

    params = pltpu.CompilerParams(vmem_limit_bytes=(16 if team == 2 else 40) * 1024 * 1024)
    cost = functools.partial(pl.CostEstimate, flops=2 * local_pairs * pair_count * width, transcendentals=0)

    paired = size == 16 and team == 2
    here = size // 2 if paired else size

    small = (vir_energy, occ_energy, pair_orbitals.T, hole_integrals)
    *energies, near_hole, own = pl.pallas_call(
        functools.partial(load_kernel, here),
        out_shape=[
            *[pltpu.VMEM(array.shape, array.dtype) for array in small],
            pltpu.VMEM((2, *amplitudes.shape), amplitudes.dtype),
        ],
        in_specs=[IN_HBM] * 6,
        out_specs=[IN_VMEM] * 5,
        scratch_shapes=[pltpu.SemaphoreType.DMA((4,)), pltpu.SemaphoreType.DMA((2,))],
        compiler_params=pltpu.CompilerParams(vmem_limit_bytes=61 * 1024 * 1024),
        cost_estimate=pl.CostEstimate(flops=0, bytes_accessed=0, transcendentals=0),
    )(*[in_hbm(array) for array in (*small, amplitudes, integrals)])

    if paired:
        early, late, owners, first_sent, last_sent = exchange_rows_16(hole_integrals, near_hole)
    else:
        early, late, owners, first_sent, last_sent = exchange_rows(hole_integrals, team)
    far_ints = [after(far, last_sent) for far in team_exchange(after(integrals, first_sent), team, size)]
    far_amps = team_exchange(after(amplitudes, first_sent), team, size)
    early, late = [[slab.reshape(-1, pair_count) for slab in slabs] for slabs in (early, late)]

    chi, own, virtual, occupied = pl.pallas_call(
        functools.partial(chi_kernel, team, here, len(early), owners),
        out_shape=[
            jax.ShapeDtypeStruct((local_pairs, pair_count), jnp.float32),
            pltpu.VMEM(own.shape, own.dtype),
            jax.ShapeDtypeStruct((IRREPS, tiles * 128), jnp.float32),
            jax.ShapeDtypeStruct((local_pairs, 128), jnp.float32),
        ],
        in_specs=[IN_HBM] * 2 + [IN_VMEM] * (3 + len(early) + team),
        out_specs=[IN_VMEM] * 4,
        scratch_shapes=[pltpu.SemaphoreType.DMA((2,))],
        input_output_aliases={2: 1},
        compiler_params=params,
        cost_estimate=cost(bytes_accessed=2 * amplitudes.nbytes),
    )(in_hbm(amplitudes), in_hbm(integrals), near(own), *energies, *early, *[near(far) for far in far_ints])
    return pl.pallas_call(
        functools.partial(update_kernel, team, len(late), owners),
        out_shape=jax.ShapeDtypeStruct((local_pairs, width), jnp.bfloat16),
        in_specs=[IN_VMEM] * (3 + len(late) + team),
        out_specs=IN_HBM,
        scratch_shapes=[
            pltpu.VMEM((local_pairs, width), jnp.bfloat16),
            pltpu.SemaphoreType.DMA((IRREPS,)),
        ],
        compiler_params=params,
        cost_estimate=cost(bytes_accessed=4 * local_pairs * width * 2),
    )(chi, virtual, occupied, *late, near(own), *[near(far) for far in far_amps])


def solution(mesh):
    size = mesh.shape["idx"]
    in_specs = (
        P(("grp", "idx"), None),
        P(("grp", "idx"), None),
        P(("grp", "idx"), None, None),
        P("grp"),
        P("grp"),
        P(("grp", "idx"), None),
    )
    out_specs = P(("grp", "idx"), None)

    def run(*args):
        return on_device(*args, size)

    return jax.shard_map(run, mesh=mesh, in_specs=in_specs, out_specs=out_specs, check_vma=False)
```

```python
import functools
import itertools
import math

import jax
import jax.numpy as jnp
from jax import lax
from jax.experimental import pallas as pl
from jax.experimental.pallas import tpu as pltpu
from jax.sharding import PartitionSpec as P

IRREPS = 8
GROUPS = 5
IN_VMEM = pl.BlockSpec(memory_space=pltpu.VMEM)
IN_HBM = pl.BlockSpec(memory_space=pltpu.HBM)


def one_hot_sum(values, columns):
    lanes = lax.broadcasted_iota(jnp.int32, (columns.shape[0], values.shape[1]), 1)
    return jnp.sum(jnp.where(lanes == columns, values, 0.0), axis=1, keepdims=True)


def occupied_sums(occ, orbitals):
    pairs = orbitals.shape[1]
    diagonal = lax.broadcasted_iota(jnp.int32, (pairs, pairs), 0) == lax.broadcasted_iota(
        jnp.int32, (pairs, pairs), 1
    )
    each = [
        one_hot_sum(occ, jnp.sum(jnp.where(diagonal, orbitals[j : j + 1, :], 0), axis=1, keepdims=True))
        for j in range(2)
    ]
    return jnp.broadcast_to(each[0] + each[1], (pairs, 128))


def irrep_tiles(block):
    return [g * block * block // 128 for g in range(IRREPS)] + [-(-IRREPS * block * block // 128)]


def virtual_sums(vir, symmetry, tiles):
    block = vir.shape[1] // IRREPS
    padded = jnp.concatenate([vir, jnp.zeros((1, 128), jnp.float32)], axis=1)
    energies = [padded[:, block * g : block * g + 128] for g in range(IRREPS)]
    first = jnp.concatenate(energies, axis=0)
    row = lax.broadcasted_iota(jnp.int32, (IRREPS, 128), 0)
    lane = lax.broadcasted_iota(jnp.int32, (IRREPS, 128), 1)
    other = jnp.bitwise_xor(row, symmetry)
    second = jnp.zeros((IRREPS, 128), jnp.float32)
    for g in range(IRREPS):
        second = jnp.where(other == g, energies[g], second)
    lead = (row * (block * block)) % 128
    sums = []
    for tile in range(tiles):
        element = jnp.clip(lane + tile * 128 - lead, 0, block * block - 1)
        least = max(0, tile * 128 - 127) // block
        a = least + sum((element >= block * (least + q)).astype(jnp.int32) for q in range(1, 3 + 254 // block))
        b = element - a * block
        sums.append(jnp.take_along_axis(first, a, axis=1) + jnp.take_along_axis(second, b, axis=1))
    starts = irrep_tiles(block)
    ends = jnp.zeros((IRREPS, 128), jnp.float32)
    for g in range(1, IRREPS):
        ends = jnp.where(row == g, sums[starts[g] - starts[g - 1]][g - 1 : g, :], ends)
    sums[0] = jnp.where(lane < lead, ends, sums[0])
    return jnp.concatenate(sums, axis=1)


def tile_copies(sources, tiles_ref, sems):
    return [pltpu.make_async_copy(source, tiles_ref.at[which], sems.at[which]) for which, source in enumerate(sources)]


def energy_sums(team, me, small, virtual_ref, occupied_ref):
    vir_ref, occ_ref, orbitals_ref = small
    virtual_ref[...] = virtual_sums(vir_ref[...].reshape(1, -1), me // team, virtual_ref.shape[1] // 128)
    occupied_ref[...] = occupied_sums(occ_ref[...].reshape(1, -1), orbitals_ref[...])


def load_kernel(team, first, *refs):
    small, sources, targets = refs[:4], refs[4:6], refs[6:10]
    tiles_ref, virtual_ref, occupied_ref, sems, tile_sems = refs[10:]
    me = lax.axis_index("idx")
    copies = [pltpu.make_async_copy(*move, sems.at[slot]) for slot, move in enumerate(zip(small, targets))]
    tiles = tile_copies(sources, tiles_ref, tile_sems)
    for copy in copies:
        copy.start()

    @pl.when(first(me))
    def _():
        for copy in tiles:
            copy.start()

    for copy in copies:
        copy.wait()

    @pl.when(first(me))
    def _():
        energy_sums(team, me, targets[:3], virtual_ref, occupied_ref)
        for copy in tiles:
            copy.wait()


def folded_dot(left, rights):
    pairs, width = left.shape
    part = width // GROUPS // 128 * 128
    rest = width - part * GROUPS
    count = sum(ref.shape[0] for ref in rights)

    def dot(spans):
        return lax.dot_general(
            jnp.concatenate([left[:, span] for span in spans], axis=0),
            jnp.concatenate([ref[:, span] for span in spans for ref in rights], axis=0),
            (((1,), (1,)), ((), ())),
            preferred_element_type=jnp.float32,
        )

    whole = dot([pl.ds(g * part, part) for g in range(GROUPS)])
    total = sum(whole[g * pairs : (g + 1) * pairs, g * count : (g + 1) * count] for g in range(GROUPS))
    return total + dot([pl.ds(part * GROUPS, rest)]) if rest else total


def bare_rows(team, pairs, stack, held, me):
    symmetry, rank = me // team, me % team
    lane = lax.broadcasted_iota(jnp.int32, (pairs, stack.shape[0]), 1)
    owner = lane
    if held is not None:
        wide = stack.shape[0] // len(held)
        owner = jnp.full(lane.shape, -1, jnp.int32)
        for slot, row in enumerate(held):
            owner = jnp.where(lane == slot * wide + symmetry, row, owner)
    pick = owner == rank * pairs + lax.broadcasted_iota(jnp.int32, lane.shape, 0)
    rows = jnp.dot(pick.astype(jnp.bfloat16), stack, preferred_element_type=jnp.float32)
    if held is None:
        return rows
    turned = rows
    for other in range(1, team):
        cut = other * pairs
        turned = jnp.where(rank == other, jnp.concatenate([rows[:, cut:], rows[:, :cut]], axis=1), turned)
    return turned


def chi_kernel(team, first, slabs, owners, amps_hbm, ints_hbm, vir_ref, occ_ref, orbitals_ref, *refs):
    bare, ints = refs[3 : slabs + 3], refs[slabs + 3 : slabs + team + 2]
    chi_ref, tiles_ref, virtual_ref, occupied_ref, sems = refs[slabs + team + 2 :]
    me = lax.axis_index("idx")

    @pl.when(jnp.logical_not(first(me)))
    def _():
        copies = tile_copies((amps_hbm, ints_hbm), tiles_ref, sems)
        for copy in copies:
            copy.start()
        energy_sums(team, me, (vir_ref, occ_ref, orbitals_ref), virtual_ref, occupied_ref)
        for copy in copies:
            copy.wait()

    chi = folded_dot(tiles_ref.at[0], [tiles_ref.at[1], *ints])
    if bare:
        stack = jnp.concatenate([ref[...] for ref in bare], axis=0)
        chi += bare_rows(team, chi_ref.shape[0], stack, owners(me)[0], me)
    chi_ref[...] = chi


def update_kernel(team, slabs, owners, chi_ref, virtual_ref, occupied_ref, *refs):
    bare, tiles_ref = refs[:slabs], refs[slabs]
    ints_ref, amps = tiles_ref.at[1], [tiles_ref.at[0], *refs[slabs + 1 : slabs + team]]
    out_ref, buffer, sems = refs[slabs + team :]
    me = lax.axis_index("idx")
    stack = jnp.concatenate([ref[...] for ref in bare], axis=0)
    mine = bare_rows(team, chi_ref.shape[0], stack, owners(me)[1], me)
    chi_half = (mine + chi_ref[...]).astype(jnp.bfloat16)
    occupied = occupied_ref[:, 0:1]
    width = ints_ref.shape[1]
    copies = []
    for g, (start, end) in enumerate(itertools.pairwise(irrep_tiles(math.isqrt(width // IRREPS)))):
        cut = pl.ds(start * 128, (end - start) * 128)
        block = jnp.concatenate([ref[:, cut] for ref in amps], axis=0)
        ladder = jnp.dot(chi_half, block, preferred_element_type=jnp.float32).astype(jnp.bfloat16)
        total = ints_ref[:, cut].astype(jnp.float32) + ladder.astype(jnp.float32)
        denominator = virtual_ref[g : g + 1, : (end - start) * 128] - occupied
        buffer[:, cut] = (total / denominator).astype(jnp.bfloat16)
        copy = pltpu.make_async_copy(buffer.at[:, cut], out_ref.at[:, cut], sems.at[g])
        copy.start()
        copies.append(copy)
    for copy in copies:
        copy.wait()


def team_exchange(block, team, size):
    return [
        lax.ppermute(block, "idx", [(d, (d // team) * team + (d - step) % team) for d in range(size)])
        for step in range(1, team)
    ]


def exchange_rows_16(hole, near_hole):
    def by_home(d, home, away):
        at_home = (d >> 3) == (d & 1)
        if isinstance(d, int):
            return d ^ (home if at_home else away)
        return d ^ jnp.where(at_home, home, away)

    def hop_one(d):
        return by_home(d, 6, 13)

    def hop_two(d):
        return by_home(d, 4, 11)

    def hop_three(d):
        return by_home(d, 8, 3)

    def from_three(d):
        return by_home(d, 3, 8)

    def permute(block, hop):
        return lax.ppermute(block, "idx", [(d, hop(d)) for d in range(16)])

    def owners(me):
        third = from_three(me)
        early, last = (me, hop_one(me)), (hop_two(me), third, hop_one(third))
        return [[row for d in pairs for row in (d, d ^ 1)] for pairs in (early, last)]

    own = jnp.concatenate([near_hole, permute(hole, lambda d: d ^ 1)], axis=0)
    first, second = permute(own, hop_one), permute(own, hop_two)
    forward = jnp.concatenate([own, first], axis=0)
    return [own, first], [second, permute(forward, hop_three)], owners, own, forward


def exchange_rows(hole, team):
    share = hole.shape[2] // team
    sent = jnp.stack([jnp.roll(hole, -rank * share, axis=2) for rank in range(team)], axis=2)
    sent = jnp.moveaxis(sent, 0, 2).reshape(IRREPS * team, *hole.shape[::2])
    received = lax.all_to_all(sent, "idx", split_axis=0, concat_axis=0, tiled=True)
    return [], [received], lambda me: (None, None), hole, received


def after(block, other):
    return lax.optimization_barrier((block, other))[0]


def on_device(amplitudes, integrals, hole_integrals, occ_energy, vir_energy, pair_orbitals, size):
    local_pairs, width = amplitudes.shape
    pair_count = hole_integrals.shape[2]
    team = pair_count // local_pairs
    block = vir_energy.shape[0] // IRREPS
    tiles = max(end - start for start, end in itertools.pairwise(irrep_tiles(block))) + 1

    def in_hbm(array):
        return pltpu.with_memory_space_constraint(array, pltpu.HBM)

    def near(array):
        return pltpu.with_memory_space_constraint(array, pltpu.VMEM) if team == 2 else array

    params = pltpu.CompilerParams(vmem_limit_bytes=(16 if team == 2 else 40) * 1024 * 1024)
    cost = functools.partial(pl.CostEstimate, flops=2 * local_pairs * pair_count * width, transcendentals=0)

    paired = size == 16 and team == 2

    def first(me):
        return jnp.logical_and(me < 8, me >> 1 != 1) if paired else me >= 0

    small = (vir_energy, occ_energy, pair_orbitals.T, hole_integrals)
    prepared = [
        pltpu.VMEM((2, *amplitudes.shape), amplitudes.dtype),
        pltpu.VMEM((IRREPS, tiles * 128), jnp.float32),
        pltpu.VMEM((local_pairs, 128), jnp.float32),
    ]
    *energies, near_hole, own, virtual, occupied = pl.pallas_call(
        functools.partial(load_kernel, team, first),
        out_shape=[*[pltpu.VMEM(array.shape, array.dtype) for array in small], *prepared],
        in_specs=[IN_HBM] * 6,
        out_specs=[IN_VMEM] * 7,
        scratch_shapes=[pltpu.SemaphoreType.DMA((4,)), pltpu.SemaphoreType.DMA((2,))],
        compiler_params=pltpu.CompilerParams(vmem_limit_bytes=61 * 1024 * 1024),
        cost_estimate=pl.CostEstimate(flops=0, bytes_accessed=0, transcendentals=0),
    )(*[in_hbm(array) for array in (*small, amplitudes, integrals)])

    if paired:
        early, late, owners, first_sent, last_sent = exchange_rows_16(hole_integrals, near_hole)
    else:
        early, late, owners, first_sent, last_sent = exchange_rows(hole_integrals, team)
    far_ints = [after(far, last_sent) for far in team_exchange(after(integrals, first_sent), team, size)]
    far_amps = team_exchange(after(amplitudes, first_sent), team, size)
    early, late = [[slab.reshape(-1, pair_count) for slab in slabs] for slabs in (early, late)]

    chi, own, virtual, occupied = pl.pallas_call(
        functools.partial(chi_kernel, team, first, len(early), owners),
        out_shape=[jax.ShapeDtypeStruct((local_pairs, pair_count), jnp.float32), *prepared],
        in_specs=[IN_HBM] * 2 + [IN_VMEM] * (5 + len(early) + team),
        out_specs=[IN_VMEM] * 4,
        scratch_shapes=[pltpu.SemaphoreType.DMA((2,))],
        input_output_aliases={5: 1, 6: 2, 7: 3},
        compiler_params=params,
        cost_estimate=cost(bytes_accessed=2 * amplitudes.nbytes),
    )(
        in_hbm(amplitudes),
        in_hbm(integrals),
        *energies,
        *[near(array) for array in (own, virtual, occupied)],
        *early,
        *[near(far) for far in far_ints],
    )
    return pl.pallas_call(
        functools.partial(update_kernel, team, len(late), owners),
        out_shape=jax.ShapeDtypeStruct((local_pairs, width), jnp.bfloat16),
        in_specs=[IN_VMEM] * (3 + len(late) + team),
        out_specs=IN_HBM,
        scratch_shapes=[
            pltpu.VMEM((local_pairs, width), jnp.bfloat16),
            pltpu.SemaphoreType.DMA((IRREPS,)),
        ],
        compiler_params=params,
        cost_estimate=cost(bytes_accessed=4 * local_pairs * width * 2),
    )(chi, virtual, occupied, *late, near(own), *[near(far) for far in far_amps])


def solution(mesh):
    size = mesh.shape["idx"]
    in_specs = (
        P(("grp", "idx"), None),
        P(("grp", "idx"), None),
        P(("grp", "idx"), None, None),
        P("grp"),
        P("grp"),
        P(("grp", "idx"), None),
    )
    out_specs = P(("grp", "idx"), None)

    def run(*args):
        return on_device(*args, size)

    return jax.shard_map(run, mesh=mesh, in_specs=in_specs, out_specs=out_specs, check_vma=False)
```

```python
import functools
import itertools
import math

import jax
import jax.numpy as jnp
from jax import lax
from jax.experimental import pallas as pl
from jax.experimental.pallas import tpu as pltpu
from jax.sharding import PartitionSpec as P

IRREPS = 8
GROUPS = 5
IN_VMEM = pl.BlockSpec(memory_space=pltpu.VMEM)
IN_HBM = pl.BlockSpec(memory_space=pltpu.HBM)


def one_hot_sum(values, columns):
    lanes = lax.broadcasted_iota(jnp.int32, (columns.shape[0], values.shape[1]), 1)
    return jnp.sum(jnp.where(lanes == columns, values, 0.0), axis=1, keepdims=True)


def occupied_sums(occ, orbitals):
    pairs = orbitals.shape[1]
    diagonal = lax.broadcasted_iota(jnp.int32, (pairs, pairs), 0) == lax.broadcasted_iota(
        jnp.int32, (pairs, pairs), 1
    )
    each = [
        one_hot_sum(occ, jnp.sum(jnp.where(diagonal, orbitals[j : j + 1, :], 0), axis=1, keepdims=True))
        for j in range(2)
    ]
    return jnp.broadcast_to(each[0] + each[1], (pairs, 128))


def irrep_tiles(block):
    return [g * block * block // 128 for g in range(IRREPS)] + [-(-IRREPS * block * block // 128)]


def virtual_sums(vir, symmetry, tiles):
    block = vir.shape[1] // IRREPS
    padded = jnp.concatenate([vir, jnp.zeros((1, 128), jnp.float32)], axis=1)
    energies = [padded[:, block * g : block * g + 128] for g in range(IRREPS)]
    first = jnp.concatenate(energies, axis=0)
    row = lax.broadcasted_iota(jnp.int32, (IRREPS, 128), 0)
    lane = lax.broadcasted_iota(jnp.int32, (IRREPS, 128), 1)
    other = jnp.bitwise_xor(row, symmetry)
    second = jnp.zeros((IRREPS, 128), jnp.float32)
    for g in range(IRREPS):
        second = jnp.where(other == g, energies[g], second)
    lead = (row * (block * block)) % 128
    sums = []
    for tile in range(tiles):
        element = jnp.clip(lane + tile * 128 - lead, 0, block * block - 1)
        least = max(0, tile * 128 - 127) // block
        a = least + sum((element >= block * (least + q)).astype(jnp.int32) for q in range(1, 3 + 254 // block))
        b = element - a * block
        sums.append(jnp.take_along_axis(first, a, axis=1) + jnp.take_along_axis(second, b, axis=1))
    starts = irrep_tiles(block)
    ends = jnp.zeros((IRREPS, 128), jnp.float32)
    for g in range(1, IRREPS):
        ends = jnp.where(row == g, sums[starts[g] - starts[g - 1]][g - 1 : g, :], ends)
    sums[0] = jnp.where(lane < lead, ends, sums[0])
    return jnp.concatenate(sums, axis=1)


def tile_copies(sources, tiles_ref, sems):
    return [pltpu.make_async_copy(source, tiles_ref.at[which], sems.at[which]) for which, source in enumerate(sources)]


def energy_sums(team, me, small, virtual_ref, occupied_ref):
    vir_ref, occ_ref, orbitals_ref = small
    virtual_ref[...] = virtual_sums(vir_ref[...].reshape(1, -1), me // team, virtual_ref.shape[1] // 128)
    occupied_ref[...] = occupied_sums(occ_ref[...].reshape(1, -1), orbitals_ref[...])


def load_kernel(team, first, *refs):
    small, sources, targets = refs[:4], refs[4:6], refs[6:10]
    tiles_ref, virtual_ref, occupied_ref, sems, tile_sems = refs[10:]
    me = lax.axis_index("idx")
    copies = [pltpu.make_async_copy(*move, sems.at[slot]) for slot, move in enumerate(zip(small, targets))]
    tiles = tile_copies(sources, tiles_ref, tile_sems)
    for copy in copies:
        copy.start()

    @pl.when(first(me))
    def _():
        for copy in tiles:
            copy.start()

    for copy in copies:
        copy.wait()

    @pl.when(first(me))
    def _():
        energy_sums(team, me, targets[:3], virtual_ref, occupied_ref)
        for copy in tiles:
            copy.wait()


def folded_dot(left, rights):
    pairs, width = left.shape
    part = width // GROUPS // 128 * 128
    rest = width - part * GROUPS
    count = sum(ref.shape[0] for ref in rights)

    def dot(spans):
        return lax.dot_general(
            jnp.concatenate([left[:, span] for span in spans], axis=0),
            jnp.concatenate([ref[:, span] for span in spans for ref in rights], axis=0),
            (((1,), (1,)), ((), ())),
            preferred_element_type=jnp.float32,
        )

    whole = dot([pl.ds(g * part, part) for g in range(GROUPS)])
    total = sum(whole[g * pairs : (g + 1) * pairs, g * count : (g + 1) * count] for g in range(GROUPS))
    return total + dot([pl.ds(part * GROUPS, rest)]) if rest else total


def bare_rows(team, pairs, stack, held, me):
    symmetry, rank = me // team, me % team
    lane = lax.broadcasted_iota(jnp.int32, (pairs, stack.shape[0]), 1)
    owner = lane
    if held is not None:
        wide = stack.shape[0] // len(held)
        owner = jnp.full(lane.shape, -1, jnp.int32)
        for slot, row in enumerate(held):
            owner = jnp.where(lane == slot * wide + symmetry, row, owner)
    pick = owner == rank * pairs + lax.broadcasted_iota(jnp.int32, lane.shape, 0)
    rows = jnp.dot(pick.astype(jnp.bfloat16), stack, preferred_element_type=jnp.float32)
    if held is None:
        return rows
    turned = rows
    for other in range(1, team):
        cut = other * pairs
        turned = jnp.where(rank == other, jnp.concatenate([rows[:, cut:], rows[:, :cut]], axis=1), turned)
    return turned


def chi_kernel(team, first, slabs, owners, amps_hbm, ints_hbm, vir_ref, occ_ref, orbitals_ref, *refs):
    bare, ints = refs[3 : slabs + 3], refs[slabs + 3 : slabs + team + 2]
    chi_ref, tiles_ref, virtual_ref, occupied_ref, sems = refs[slabs + team + 2 :]
    me = lax.axis_index("idx")

    @pl.when(jnp.logical_not(first(me)))
    def _():
        copies = tile_copies((amps_hbm, ints_hbm), tiles_ref, sems)
        for copy in copies:
            copy.start()
        energy_sums(team, me, (vir_ref, occ_ref, orbitals_ref), virtual_ref, occupied_ref)
        for copy in copies:
            copy.wait()

    chi = folded_dot(tiles_ref.at[0], [tiles_ref.at[1], *ints])
    if bare:
        stack = jnp.concatenate([ref[...] for ref in bare], axis=0)
        chi += bare_rows(team, chi_ref.shape[0], stack, owners(me)[0], me)
    chi_ref[...] = chi


def update_kernel(team, slabs, owners, chi_ref, virtual_ref, occupied_ref, *refs):
    bare, tiles_ref = refs[:slabs], refs[slabs]
    ints_ref, amps = tiles_ref.at[1], [tiles_ref.at[0], *refs[slabs + 1 : slabs + team]]
    out_ref, buffer, sems = refs[slabs + team :]
    me = lax.axis_index("idx")
    stack = jnp.concatenate([ref[...] for ref in bare], axis=0)
    mine = bare_rows(team, chi_ref.shape[0], stack, owners(me)[1], me)
    chi_half = (mine + chi_ref[...]).astype(jnp.bfloat16)
    occupied = occupied_ref[:, 0:1]
    width = ints_ref.shape[1]
    copies = []
    for g, (start, end) in enumerate(itertools.pairwise(irrep_tiles(math.isqrt(width // IRREPS)))):
        cut = pl.ds(start * 128, (end - start) * 128)
        block = jnp.concatenate([ref[:, cut] for ref in amps], axis=0)
        ladder = jnp.dot(chi_half, block, preferred_element_type=jnp.float32)
        total = ints_ref[:, cut].astype(jnp.float32) + ladder
        denominator = virtual_ref[g : g + 1, : (end - start) * 128] - occupied
        buffer[:, cut] = (total / denominator).astype(jnp.bfloat16)
        copy = pltpu.make_async_copy(buffer.at[:, cut], out_ref.at[:, cut], sems.at[g])
        copy.start()
        copies.append(copy)
    for copy in copies:
        copy.wait()


def team_exchange(block, team, size):
    return [
        lax.ppermute(block, "idx", [(d, (d // team) * team + (d - step) % team) for d in range(size)])
        for step in range(1, team)
    ]


def exchange_rows_16(hole, near_hole):
    def by_home(d, home, away):
        at_home = (d >> 3) == (d & 1)
        if isinstance(d, int):
            return d ^ (home if at_home else away)
        return d ^ jnp.where(at_home, home, away)

    def hop_one(d):
        return by_home(d, 6, 13)

    def hop_two(d):
        return by_home(d, 4, 11)

    def hop_three(d):
        return by_home(d, 8, 3)

    def from_three(d):
        return by_home(d, 3, 8)

    def permute(block, hop):
        return lax.ppermute(block, "idx", [(d, hop(d)) for d in range(16)])

    def owners(me):
        third = from_three(me)
        early, last = (me, hop_one(me)), (hop_two(me), third, hop_one(third))
        return [[row for d in pairs for row in (d, d ^ 1)] for pairs in (early, last)]

    own = jnp.concatenate([near_hole, permute(hole, lambda d: d ^ 1)], axis=0)
    first, second = permute(own, hop_one), permute(own, hop_two)
    forward = jnp.concatenate([own, first], axis=0)
    return [own, first], [second, permute(forward, hop_three)], owners, own, forward


def exchange_rows(hole, team):
    share = hole.shape[2] // team
    sent = jnp.stack([jnp.roll(hole, -rank * share, axis=2) for rank in range(team)], axis=2)
    sent = jnp.moveaxis(sent, 0, 2).reshape(IRREPS * team, *hole.shape[::2])
    received = lax.all_to_all(sent, "idx", split_axis=0, concat_axis=0, tiled=True)
    return [], [received], lambda me: (None, None), hole, received


def after(block, other):
    return lax.optimization_barrier((block, other))[0]


def on_device(amplitudes, integrals, hole_integrals, occ_energy, vir_energy, pair_orbitals, size):
    local_pairs, width = amplitudes.shape
    pair_count = hole_integrals.shape[2]
    team = pair_count // local_pairs
    block = vir_energy.shape[0] // IRREPS
    tiles = max(end - start for start, end in itertools.pairwise(irrep_tiles(block))) + 1

    def in_hbm(array):
        return pltpu.with_memory_space_constraint(array, pltpu.HBM)

    def near(array):
        return pltpu.with_memory_space_constraint(array, pltpu.VMEM) if team == 2 else array

    params = pltpu.CompilerParams(vmem_limit_bytes=(16 if team == 2 else 40) * 1024 * 1024)
    cost = functools.partial(pl.CostEstimate, flops=2 * local_pairs * pair_count * width, transcendentals=0)

    paired = size == 16 and team == 2

    def first(me):
        return jnp.logical_and(me < 8, me >> 1 != 1) if paired else me >= 0

    small = (vir_energy, occ_energy, pair_orbitals.T, hole_integrals)
    prepared = [
        pltpu.VMEM((2, *amplitudes.shape), amplitudes.dtype),
        pltpu.VMEM((IRREPS, tiles * 128), jnp.float32),
        pltpu.VMEM((local_pairs, 128), jnp.float32),
    ]
    *energies, near_hole, own, virtual, occupied = pl.pallas_call(
        functools.partial(load_kernel, team, first),
        out_shape=[*[pltpu.VMEM(array.shape, array.dtype) for array in small], *prepared],
        in_specs=[IN_HBM] * 6,
        out_specs=[IN_VMEM] * 7,
        scratch_shapes=[pltpu.SemaphoreType.DMA((4,)), pltpu.SemaphoreType.DMA((2,))],
        compiler_params=pltpu.CompilerParams(vmem_limit_bytes=61 * 1024 * 1024),
        cost_estimate=pl.CostEstimate(flops=0, bytes_accessed=0, transcendentals=0),
    )(*[in_hbm(array) for array in (*small, amplitudes, integrals)])

    if paired:
        early, late, owners, first_sent, last_sent = exchange_rows_16(hole_integrals, near_hole)
    else:
        early, late, owners, first_sent, last_sent = exchange_rows(hole_integrals, team)
    far_ints = [after(far, last_sent) for far in team_exchange(after(integrals, first_sent), team, size)]
    far_amps = team_exchange(after(amplitudes, first_sent), team, size)
    early, late = [[slab.reshape(-1, pair_count) for slab in slabs] for slabs in (early, late)]

    chi, own, virtual, occupied = pl.pallas_call(
        functools.partial(chi_kernel, team, first, len(early), owners),
        out_shape=[jax.ShapeDtypeStruct((local_pairs, pair_count), jnp.float32), *prepared],
        in_specs=[IN_HBM] * 2 + [IN_VMEM] * (5 + len(early) + team),
        out_specs=[IN_VMEM] * 4,
        scratch_shapes=[pltpu.SemaphoreType.DMA((2,))],
        input_output_aliases={5: 1, 6: 2, 7: 3},
        compiler_params=params,
        cost_estimate=cost(bytes_accessed=2 * amplitudes.nbytes),
    )(
        in_hbm(amplitudes),
        in_hbm(integrals),
        *energies,
        *[near(array) for array in (own, virtual, occupied)],
        *early,
        *[near(far) for far in far_ints],
    )
    return pl.pallas_call(
        functools.partial(update_kernel, team, len(late), owners),
        out_shape=jax.ShapeDtypeStruct((local_pairs, width), jnp.bfloat16),
        in_specs=[IN_VMEM] * (3 + len(late) + team),
        out_specs=IN_HBM,
        scratch_shapes=[
            pltpu.VMEM((local_pairs, width), jnp.bfloat16),
            pltpu.SemaphoreType.DMA((IRREPS,)),
        ],
        compiler_params=params,
        cost_estimate=cost(bytes_accessed=4 * local_pairs * width * 2),
    )(chi, virtual, occupied, *late, near(own), *[near(far) for far in far_amps])


def solution(mesh):
    size = mesh.shape["idx"]
    in_specs = (
        P(("grp", "idx"), None),
        P(("grp", "idx"), None),
        P(("grp", "idx"), None, None),
        P("grp"),
        P("grp"),
        P(("grp", "idx"), None),
    )
    out_specs = P(("grp", "idx"), None)

    def run(*args):
        return on_device(*args, size)

    return jax.shard_map(run, mesh=mesh, in_specs=in_specs, out_specs=out_specs, check_vma=False)
```

```python
import functools
import itertools
import math

import jax
import jax.numpy as jnp
from jax import lax
from jax.experimental import pallas as pl
from jax.experimental.pallas import tpu as pltpu
from jax.sharding import PartitionSpec as P

IRREPS = 8
GROUPS = 5
IN_VMEM = pl.BlockSpec(memory_space=pltpu.VMEM)
IN_HBM = pl.BlockSpec(memory_space=pltpu.HBM)


def one_hot_sum(values, columns):
    lanes = lax.broadcasted_iota(jnp.int32, (columns.shape[0], values.shape[1]), 1)
    return jnp.sum(jnp.where(lanes == columns, values, 0.0), axis=1, keepdims=True)


def occupied_sums(occ, orbitals):
    pairs = orbitals.shape[1]
    diagonal = lax.broadcasted_iota(jnp.int32, (pairs, pairs), 0) == lax.broadcasted_iota(
        jnp.int32, (pairs, pairs), 1
    )
    each = [
        one_hot_sum(occ, jnp.sum(jnp.where(diagonal, orbitals[j : j + 1, :], 0), axis=1, keepdims=True))
        for j in range(2)
    ]
    return jnp.broadcast_to(each[0] + each[1], (pairs, 128))


def irrep_tiles(block):
    return [g * block * block // 128 for g in range(IRREPS)] + [-(-IRREPS * block * block // 128)]


def virtual_sums(vir, symmetry, tiles):
    block = vir.shape[1] // IRREPS
    padded = jnp.concatenate([vir, jnp.zeros((1, 128), jnp.float32)], axis=1)
    energies = [padded[:, block * g : block * g + 128] for g in range(IRREPS)]
    first = jnp.concatenate(energies, axis=0)
    row = lax.broadcasted_iota(jnp.int32, (IRREPS, 128), 0)
    lane = lax.broadcasted_iota(jnp.int32, (IRREPS, 128), 1)
    other = jnp.bitwise_xor(row, symmetry)
    second = jnp.zeros((IRREPS, 128), jnp.float32)
    for g in range(IRREPS):
        second = jnp.where(other == g, energies[g], second)
    lead = (row * (block * block)) % 128
    sums = []
    for tile in range(tiles):
        element = jnp.clip(lane + tile * 128 - lead, 0, block * block - 1)
        least = max(0, tile * 128 - 127) // block
        a = least + sum((element >= block * (least + q)).astype(jnp.int32) for q in range(1, 3 + 254 // block))
        b = element - a * block
        sums.append(jnp.take_along_axis(first, a, axis=1) + jnp.take_along_axis(second, b, axis=1))
    starts = irrep_tiles(block)
    ends = jnp.zeros((IRREPS, 128), jnp.float32)
    for g in range(1, IRREPS):
        ends = jnp.where(row == g, sums[starts[g] - starts[g - 1]][g - 1 : g, :], ends)
    sums[0] = jnp.where(lane < lead, ends, sums[0])
    return jnp.concatenate(sums, axis=1)


def tile_copies(sources, tiles_ref, sems):
    return [pltpu.make_async_copy(source, tiles_ref.at[which], sems.at[which]) for which, source in enumerate(sources)]


def energy_sums(team, me, small, virtual_ref, occupied_ref):
    vir_ref, occ_ref, orbitals_ref = small
    virtual_ref[...] = virtual_sums(vir_ref[...].reshape(1, -1), me // team, virtual_ref.shape[1] // 128)
    occupied_ref[...] = occupied_sums(occ_ref[...].reshape(1, -1), orbitals_ref[...])


def load_kernel(team, first, *refs):
    small, sources, targets = refs[:4], refs[4:6], refs[6:10]
    tiles_ref, virtual_ref, occupied_ref, sems, tile_sems = refs[10:]
    me = lax.axis_index("idx")
    copies = [pltpu.make_async_copy(*move, sems.at[slot]) for slot, move in enumerate(zip(small, targets))]
    tiles = tile_copies(sources, tiles_ref, tile_sems)
    for copy in copies:
        copy.start()

    @pl.when(first(me))
    def _():
        for copy in tiles:
            copy.start()

    for copy in copies:
        copy.wait()

    @pl.when(first(me))
    def _():
        energy_sums(team, me, targets[:3], virtual_ref, occupied_ref)
        for copy in tiles:
            copy.wait()


def folded_dot(left, rights):
    pairs, width = left.shape
    part = width // GROUPS // 128 * 128
    rest = width - part * GROUPS
    count = sum(ref.shape[0] for ref in rights)

    def dot(spans):
        return lax.dot_general(
            jnp.concatenate([left[:, span] for span in spans], axis=0),
            jnp.concatenate([ref[:, span] for span in spans for ref in rights], axis=0),
            (((1,), (1,)), ((), ())),
            preferred_element_type=jnp.float32,
        )

    whole = dot([pl.ds(g * part, part) for g in range(GROUPS)])
    total = sum(whole[g * pairs : (g + 1) * pairs, g * count : (g + 1) * count] for g in range(GROUPS))
    return total + dot([pl.ds(part * GROUPS, rest)]) if rest else total


def bare_rows(team, pairs, stack, held, me):
    symmetry, rank = me // team, me % team
    if held is None:
        lane = lax.broadcasted_iota(jnp.int32, (pairs, stack.shape[0]), 1)
        pick = lane == rank * pairs + lax.broadcasted_iota(jnp.int32, lane.shape, 0)
        return jnp.dot(pick.astype(jnp.bfloat16), stack, preferred_element_type=jnp.float32)
    wide = stack.shape[0] // len(held)
    values = stack.astype(jnp.float32)
    place = lax.broadcasted_iota(jnp.int32, (wide, stack.shape[1]), 0)
    target = lax.broadcasted_iota(jnp.int32, (pairs, stack.shape[1]), 0) + rank * pairs
    rows = jnp.zeros(target.shape, jnp.float32)
    for slot, row in enumerate(held):
        here = values[slot * wide : (slot + 1) * wide]
        here = jnp.sum(jnp.where(place == symmetry, here, 0.0), axis=0, keepdims=True)
        rows = jnp.where(target == row, here, rows)
    turned = rows
    for other in range(1, team):
        cut = other * pairs
        turned = jnp.where(rank == other, jnp.concatenate([rows[:, cut:], rows[:, :cut]], axis=1), turned)
    return turned


def chi_kernel(team, first, slabs, owners, amps_hbm, ints_hbm, vir_ref, occ_ref, orbitals_ref, *refs):
    bare, ints = refs[3 : slabs + 3], refs[slabs + 3 : slabs + team + 2]
    chi_ref, tiles_ref, virtual_ref, occupied_ref, sems = refs[slabs + team + 2 :]
    me = lax.axis_index("idx")

    @pl.when(jnp.logical_not(first(me)))
    def _():
        copies = tile_copies((amps_hbm, ints_hbm), tiles_ref, sems)
        for copy in copies:
            copy.start()
        energy_sums(team, me, (vir_ref, occ_ref, orbitals_ref), virtual_ref, occupied_ref)
        for copy in copies:
            copy.wait()

    chi = folded_dot(tiles_ref.at[0], [tiles_ref.at[1], *ints])
    if bare:
        stack = jnp.concatenate([ref[...] for ref in bare], axis=0)
        chi += bare_rows(team, chi_ref.shape[0], stack, owners(me)[0], me)
    chi_ref[...] = chi


def update_kernel(team, slabs, owners, chi_ref, virtual_ref, occupied_ref, *refs):
    bare, tiles_ref = refs[:slabs], refs[slabs]
    ints_ref, amps = tiles_ref.at[1], [tiles_ref.at[0], *refs[slabs + 1 : slabs + team]]
    out_ref, buffer, sems = refs[slabs + team :]
    me = lax.axis_index("idx")
    stack = jnp.concatenate([ref[...] for ref in bare], axis=0)
    mine = bare_rows(team, chi_ref.shape[0], stack, owners(me)[1], me)
    chi_half = (mine + chi_ref[...]).astype(jnp.bfloat16)
    occupied = occupied_ref[:, 0:1]
    width = ints_ref.shape[1]
    copies = []
    for g, (start, end) in enumerate(itertools.pairwise(irrep_tiles(math.isqrt(width // IRREPS)))):
        cut = pl.ds(start * 128, (end - start) * 128)
        block = jnp.concatenate([ref[:, cut] for ref in amps], axis=0)
        ladder = jnp.dot(chi_half, block, preferred_element_type=jnp.float32)
        total = ints_ref[:, cut].astype(jnp.float32) + ladder
        denominator = virtual_ref[g : g + 1, : (end - start) * 128] - occupied
        buffer[:, cut] = (total / denominator).astype(jnp.bfloat16)
        copy = pltpu.make_async_copy(buffer.at[:, cut], out_ref.at[:, cut], sems.at[g])
        copy.start()
        copies.append(copy)
    for copy in copies:
        copy.wait()


def team_exchange(block, team, size):
    return [
        lax.ppermute(block, "idx", [(d, (d // team) * team + (d - step) % team) for d in range(size)])
        for step in range(1, team)
    ]


def exchange_rows_16(hole, near_hole):
    def by_home(d, home, away):
        at_home = (d >> 3) == (d & 1)
        if isinstance(d, int):
            return d ^ (home if at_home else away)
        return d ^ jnp.where(at_home, home, away)

    def hop_one(d):
        return by_home(d, 6, 13)

    def hop_two(d):
        return by_home(d, 4, 11)

    def hop_three(d):
        return by_home(d, 8, 3)

    def from_three(d):
        return by_home(d, 3, 8)

    def permute(block, hop):
        return lax.ppermute(block, "idx", [(d, hop(d)) for d in range(16)])

    def owners(me):
        third = from_three(me)
        early, last = (me, hop_one(me)), (hop_two(me), third, hop_one(third))
        return [[row for d in pairs for row in (d, d ^ 1)] for pairs in (early, last)]

    own = jnp.concatenate([near_hole, permute(hole, lambda d: d ^ 1)], axis=0)
    first, second = permute(own, hop_one), permute(own, hop_two)
    forward = jnp.concatenate([own, first], axis=0)
    return [own, first], [second, permute(forward, hop_three)], owners, own, forward


def exchange_rows(hole, team):
    share = hole.shape[2] // team
    sent = jnp.stack([jnp.roll(hole, -rank * share, axis=2) for rank in range(team)], axis=2)
    sent = jnp.moveaxis(sent, 0, 2).reshape(IRREPS * team, *hole.shape[::2])
    received = lax.all_to_all(sent, "idx", split_axis=0, concat_axis=0, tiled=True)
    return [], [received], lambda me: (None, None), hole, received


def after(block, other):
    return lax.optimization_barrier((block, other))[0]


def on_device(amplitudes, integrals, hole_integrals, occ_energy, vir_energy, pair_orbitals, size):
    local_pairs, width = amplitudes.shape
    pair_count = hole_integrals.shape[2]
    team = pair_count // local_pairs
    block = vir_energy.shape[0] // IRREPS
    tiles = max(end - start for start, end in itertools.pairwise(irrep_tiles(block))) + 1

    def in_hbm(array):
        return pltpu.with_memory_space_constraint(array, pltpu.HBM)

    def near(array):
        return pltpu.with_memory_space_constraint(array, pltpu.VMEM) if team == 2 else array

    params = pltpu.CompilerParams(vmem_limit_bytes=(16 if team == 2 else 40) * 1024 * 1024)
    cost = functools.partial(pl.CostEstimate, flops=2 * local_pairs * pair_count * width, transcendentals=0)

    paired = size == 16 and team == 2

    def first(me):
        return jnp.logical_and(me < 8, me >> 1 != 1) if paired else me >= 0

    small = (vir_energy, occ_energy, pair_orbitals.T, hole_integrals)
    prepared = [
        pltpu.VMEM((2, *amplitudes.shape), amplitudes.dtype),
        pltpu.VMEM((IRREPS, tiles * 128), jnp.float32),
        pltpu.VMEM((local_pairs, 128), jnp.float32),
    ]
    *energies, near_hole, own, virtual, occupied = pl.pallas_call(
        functools.partial(load_kernel, team, first),
        out_shape=[*[pltpu.VMEM(array.shape, array.dtype) for array in small], *prepared],
        in_specs=[IN_HBM] * 6,
        out_specs=[IN_VMEM] * 7,
        scratch_shapes=[pltpu.SemaphoreType.DMA((4,)), pltpu.SemaphoreType.DMA((2,))],
        compiler_params=pltpu.CompilerParams(vmem_limit_bytes=61 * 1024 * 1024),
        cost_estimate=pl.CostEstimate(flops=0, bytes_accessed=0, transcendentals=0),
    )(*[in_hbm(array) for array in (*small, amplitudes, integrals)])

    if paired:
        early, late, owners, first_sent, last_sent = exchange_rows_16(hole_integrals, near_hole)
    else:
        early, late, owners, first_sent, last_sent = exchange_rows(hole_integrals, team)
    far_ints = [after(far, last_sent) for far in team_exchange(after(integrals, first_sent), team, size)]
    far_amps = team_exchange(after(amplitudes, first_sent), team, size)
    early, late = [[slab.reshape(-1, pair_count) for slab in slabs] for slabs in (early, late)]

    chi, own, virtual, occupied = pl.pallas_call(
        functools.partial(chi_kernel, team, first, len(early), owners),
        out_shape=[jax.ShapeDtypeStruct((local_pairs, pair_count), jnp.float32), *prepared],
        in_specs=[IN_HBM] * 2 + [IN_VMEM] * (5 + len(early) + team),
        out_specs=[IN_VMEM] * 4,
        scratch_shapes=[pltpu.SemaphoreType.DMA((2,))],
        input_output_aliases={5: 1, 6: 2, 7: 3},
        compiler_params=params,
        cost_estimate=cost(bytes_accessed=2 * amplitudes.nbytes),
    )(
        in_hbm(amplitudes),
        in_hbm(integrals),
        *energies,
        *[near(array) for array in (own, virtual, occupied)],
        *early,
        *[near(far) for far in far_ints],
    )
    return pl.pallas_call(
        functools.partial(update_kernel, team, len(late), owners),
        out_shape=jax.ShapeDtypeStruct((local_pairs, width), jnp.bfloat16),
        in_specs=[IN_VMEM] * (3 + len(late) + team),
        out_specs=IN_HBM,
        scratch_shapes=[
            pltpu.VMEM((local_pairs, width), jnp.bfloat16),
            pltpu.SemaphoreType.DMA((IRREPS,)),
        ],
        compiler_params=params,
        cost_estimate=cost(bytes_accessed=4 * local_pairs * width * 2),
    )(chi, virtual, occupied, *late, near(own), *[near(far) for far in far_amps])


def solution(mesh):
    size = mesh.shape["idx"]
    in_specs = (
        P(("grp", "idx"), None),
        P(("grp", "idx"), None),
        P(("grp", "idx"), None, None),
        P("grp"),
        P("grp"),
        P(("grp", "idx"), None),
    )
    out_specs = P(("grp", "idx"), None)

    def run(*args):
        return on_device(*args, size)

    return jax.shard_map(run, mesh=mesh, in_specs=in_specs, out_specs=out_specs, check_vma=False)
```

```python
import functools
import itertools
import math

import jax
import jax.numpy as jnp
from jax import lax
from jax.experimental import pallas as pl
from jax.experimental.pallas import tpu as pltpu
from jax.sharding import PartitionSpec as P

IRREPS = 8
GROUPS = 5
IN_VMEM = pl.BlockSpec(memory_space=pltpu.VMEM)
IN_HBM = pl.BlockSpec(memory_space=pltpu.HBM)


def one_hot_sum(values, columns):
    lanes = lax.broadcasted_iota(jnp.int32, (columns.shape[0], values.shape[1]), 1)
    return jnp.sum(jnp.where(lanes == columns, values, 0.0), axis=1, keepdims=True)


def occupied_sums(occ, orbitals):
    pairs = orbitals.shape[1]
    diagonal = lax.broadcasted_iota(jnp.int32, (pairs, pairs), 0) == lax.broadcasted_iota(
        jnp.int32, (pairs, pairs), 1
    )
    each = [
        one_hot_sum(occ, jnp.sum(jnp.where(diagonal, orbitals[j : j + 1, :], 0), axis=1, keepdims=True))
        for j in range(2)
    ]
    return jnp.broadcast_to(each[0] + each[1], (pairs, 128))


def irrep_tiles(block):
    return [g * block * block // 128 for g in range(IRREPS)] + [-(-IRREPS * block * block // 128)]


def virtual_sums(vir, symmetry, tiles):
    block = vir.shape[1] // IRREPS
    padded = jnp.concatenate([vir, jnp.zeros((1, 128), jnp.float32)], axis=1)
    energies = [padded[:, block * g : block * g + 128] for g in range(IRREPS)]
    first = jnp.concatenate(energies, axis=0)
    row = lax.broadcasted_iota(jnp.int32, (IRREPS, 128), 0)
    lane = lax.broadcasted_iota(jnp.int32, (IRREPS, 128), 1)
    other = jnp.bitwise_xor(row, symmetry)
    second = jnp.zeros((IRREPS, 128), jnp.float32)
    for g in range(IRREPS):
        second = jnp.where(other == g, energies[g], second)
    lead = (row * (block * block)) % 128
    sums = []
    for tile in range(tiles):
        element = jnp.clip(lane + tile * 128 - lead, 0, block * block - 1)
        least = max(0, tile * 128 - 127) // block
        a = least + sum((element >= block * (least + q)).astype(jnp.int32) for q in range(1, 3 + 254 // block))
        b = element - a * block
        sums.append(jnp.take_along_axis(first, a, axis=1) + jnp.take_along_axis(second, b, axis=1))
    starts = irrep_tiles(block)
    ends = jnp.zeros((IRREPS, 128), jnp.float32)
    for g in range(1, IRREPS):
        ends = jnp.where(row == g, sums[starts[g] - starts[g - 1]][g - 1 : g, :], ends)
    sums[0] = jnp.where(lane < lead, ends, sums[0])
    return jnp.concatenate(sums, axis=1)


def tile_copies(sources, tiles_ref, sems):
    return [pltpu.make_async_copy(source, tiles_ref.at[which], sems.at[which]) for which, source in enumerate(sources)]


def energy_sums(team, me, small, virtual_ref, occupied_ref):
    vir_ref, occ_ref, orbitals_ref = small
    virtual_ref[...] = virtual_sums(vir_ref[...].reshape(1, -1), me // team, virtual_ref.shape[1] // 128)
    occupied_ref[...] = occupied_sums(occ_ref[...].reshape(1, -1), orbitals_ref[...])


def load_kernel(team, first, *refs):
    small, sources, targets = refs[:4], refs[4:6], refs[6:10]
    tiles_ref, virtual_ref, occupied_ref, sems, tile_sems = refs[10:]
    me = lax.axis_index("idx")
    copies = [pltpu.make_async_copy(*move, sems.at[slot]) for slot, move in enumerate(zip(small, targets))]
    tiles = tile_copies(sources, tiles_ref, tile_sems)
    for copy in copies:
        copy.start()

    @pl.when(first(me))
    def _():
        for copy in tiles:
            copy.start()

    for copy in copies:
        copy.wait()

    @pl.when(first(me))
    def _():
        energy_sums(team, me, targets[:3], virtual_ref, occupied_ref)
        for copy in tiles:
            copy.wait()


def folded_dot(left, rights):
    pairs, width = left.shape
    part = width // GROUPS // 128 * 128
    rest = width - part * GROUPS
    count = sum(ref.shape[0] for ref in rights)

    def dot(spans):
        return lax.dot_general(
            jnp.concatenate([left[:, span] for span in spans], axis=0),
            jnp.concatenate([ref[:, span] for span in spans for ref in rights], axis=0),
            (((1,), (1,)), ((), ())),
            preferred_element_type=jnp.float32,
        )

    whole = dot([pl.ds(g * part, part) for g in range(GROUPS)])
    total = sum(whole[g * pairs : (g + 1) * pairs, g * count : (g + 1) * count] for g in range(GROUPS))
    return total + dot([pl.ds(part * GROUPS, rest)]) if rest else total


def bare_rows(team, pairs, stack, held, me):
    symmetry, rank = me // team, me % team
    if held is None:
        lane = lax.broadcasted_iota(jnp.int32, (pairs, stack.shape[0]), 1)
        pick = lane == rank * pairs + lax.broadcasted_iota(jnp.int32, lane.shape, 0)
        return jnp.dot(pick.astype(jnp.bfloat16), stack, preferred_element_type=jnp.float32)
    wide = stack.shape[0] // len(held)
    values = stack.astype(jnp.float32)
    target = lax.broadcasted_iota(jnp.int32, (pairs, stack.shape[1]), 0) + rank * pairs
    rows = jnp.zeros(target.shape, jnp.float32)
    for slot, row in enumerate(held):
        here = values[slot * wide : (slot + 1) * wide]
        rows = jnp.where(target == row, pltpu.roll(here, (row - symmetry) & (wide - 1), 0), rows)
    turned = rows
    for other in range(1, team):
        cut = other * pairs
        turned = jnp.where(rank == other, jnp.concatenate([rows[:, cut:], rows[:, :cut]], axis=1), turned)
    return turned


def chi_kernel(team, first, slabs, owners, amps_hbm, ints_hbm, vir_ref, occ_ref, orbitals_ref, *refs):
    bare, ints = refs[3 : slabs + 3], refs[slabs + 3 : slabs + team + 2]
    chi_ref, tiles_ref, virtual_ref, occupied_ref, sems = refs[slabs + team + 2 :]
    me = lax.axis_index("idx")

    @pl.when(jnp.logical_not(first(me)))
    def _():
        copies = tile_copies((amps_hbm, ints_hbm), tiles_ref, sems)
        for copy in copies:
            copy.start()
        energy_sums(team, me, (vir_ref, occ_ref, orbitals_ref), virtual_ref, occupied_ref)
        for copy in copies:
            copy.wait()

    chi = folded_dot(tiles_ref.at[0], [tiles_ref.at[1], *ints])
    if bare:
        stack = jnp.concatenate([ref[...] for ref in bare], axis=0)
        chi += bare_rows(team, chi_ref.shape[0], stack, owners(me)[0], me)
    chi_ref[...] = chi


def update_kernel(team, slabs, owners, chi_ref, virtual_ref, occupied_ref, *refs):
    bare, tiles_ref = refs[:slabs], refs[slabs]
    ints_ref, amps = tiles_ref.at[1], [tiles_ref.at[0], *refs[slabs + 1 : slabs + team]]
    out_ref, buffer, sems = refs[slabs + team :]
    me = lax.axis_index("idx")
    stack = jnp.concatenate([ref[...] for ref in bare], axis=0)
    mine = bare_rows(team, chi_ref.shape[0], stack, owners(me)[1], me)
    chi_half = (mine + chi_ref[...]).astype(jnp.bfloat16)
    occupied = occupied_ref[:, 0:1]
    width = ints_ref.shape[1]
    copies = []
    for g, (start, end) in enumerate(itertools.pairwise(irrep_tiles(math.isqrt(width // IRREPS)))):
        parts = [(start, end)] if g < IRREPS - 1 else [(start, (start + 2 * end) // 3), ((start + 2 * end) // 3, end)]
        for part, (low, high) in enumerate(parts):
            cut = pl.ds(low * 128, (high - low) * 128)
            block = jnp.concatenate([ref[:, cut] for ref in amps], axis=0)
            ladder = jnp.dot(chi_half, block, preferred_element_type=jnp.float32)
            total = ints_ref[:, cut].astype(jnp.float32) + ladder
            denominator = virtual_ref[g : g + 1, (low - start) * 128 : (high - start) * 128] - occupied
            buffer[:, cut] = (total / denominator).astype(jnp.bfloat16)
            copy = pltpu.make_async_copy(buffer.at[:, cut], out_ref.at[:, cut], sems.at[g + part])
            copy.start()
            copies.append(copy)
    for copy in copies:
        copy.wait()


def team_exchange(block, team, size):
    return [
        lax.ppermute(block, "idx", [(d, (d // team) * team + (d - step) % team) for d in range(size)])
        for step in range(1, team)
    ]


def exchange_rows_16(hole, near_hole):
    def by_home(d, home, away):
        at_home = (d >> 3) == (d & 1)
        if isinstance(d, int):
            return d ^ (home if at_home else away)
        return d ^ jnp.where(at_home, home, away)

    def hop_one(d):
        return by_home(d, 6, 13)

    def hop_two(d):
        return by_home(d, 4, 11)

    def hop_three(d):
        return by_home(d, 8, 3)

    def from_three(d):
        return by_home(d, 3, 8)

    def permute(block, hop):
        return lax.ppermute(block, "idx", [(d, hop(d)) for d in range(16)])

    def owners(me):
        third = from_three(me)
        early, last = (me, hop_one(me)), (hop_two(me), third, hop_one(third))
        return [[row for d in pairs for row in (d, d ^ 1)] for pairs in (early, last)]

    own = jnp.concatenate([near_hole, permute(hole, lambda d: d ^ 1)], axis=0)
    first, second = permute(own, hop_one), permute(own, hop_two)
    forward = jnp.concatenate([own, first], axis=0)
    return [own, first], [second, permute(forward, hop_three)], owners, own, forward


def exchange_rows(hole, team):
    share = hole.shape[2] // team
    sent = jnp.stack([jnp.roll(hole, -rank * share, axis=2) for rank in range(team)], axis=2)
    sent = jnp.moveaxis(sent, 0, 2).reshape(IRREPS * team, *hole.shape[::2])
    received = lax.all_to_all(sent, "idx", split_axis=0, concat_axis=0, tiled=True)
    return [], [received], lambda me: (None, None), hole, received


def after(block, other):
    return lax.optimization_barrier((block, other))[0]


def on_device(amplitudes, integrals, hole_integrals, occ_energy, vir_energy, pair_orbitals, size):
    local_pairs, width = amplitudes.shape
    pair_count = hole_integrals.shape[2]
    team = pair_count // local_pairs
    block = vir_energy.shape[0] // IRREPS
    tiles = max(end - start for start, end in itertools.pairwise(irrep_tiles(block))) + 1

    def in_hbm(array):
        return pltpu.with_memory_space_constraint(array, pltpu.HBM)

    def near(array):
        return pltpu.with_memory_space_constraint(array, pltpu.VMEM) if team == 2 else array

    params = pltpu.CompilerParams(vmem_limit_bytes=(16 if team == 2 else 40) * 1024 * 1024)
    cost = functools.partial(pl.CostEstimate, flops=2 * local_pairs * pair_count * width, transcendentals=0)

    paired = size == 16 and team == 2

    def first(me):
        return jnp.logical_and(me < 8, me >> 1 != 1) if paired else me >= 0

    small = (vir_energy, occ_energy, pair_orbitals.T, hole_integrals)
    prepared = [
        pltpu.VMEM((2, *amplitudes.shape), amplitudes.dtype),
        pltpu.VMEM((IRREPS, tiles * 128), jnp.float32),
        pltpu.VMEM((local_pairs, 128), jnp.float32),
    ]
    *energies, near_hole, own, virtual, occupied = pl.pallas_call(
        functools.partial(load_kernel, team, first),
        out_shape=[*[pltpu.VMEM(array.shape, array.dtype) for array in small], *prepared],
        in_specs=[IN_HBM] * 6,
        out_specs=[IN_VMEM] * 7,
        scratch_shapes=[pltpu.SemaphoreType.DMA((4,)), pltpu.SemaphoreType.DMA((2,))],
        compiler_params=pltpu.CompilerParams(vmem_limit_bytes=61 * 1024 * 1024),
        cost_estimate=pl.CostEstimate(flops=0, bytes_accessed=0, transcendentals=0),
    )(*[in_hbm(array) for array in (*small, amplitudes, integrals)])

    if paired:
        early, late, owners, first_sent, last_sent = exchange_rows_16(hole_integrals, near_hole)
    else:
        early, late, owners, first_sent, last_sent = exchange_rows(hole_integrals, team)
    far_ints = [after(far, last_sent) for far in team_exchange(after(integrals, first_sent), team, size)]
    far_amps = team_exchange(after(amplitudes, first_sent), team, size)
    early, late = [[slab.reshape(-1, pair_count) for slab in slabs] for slabs in (early, late)]

    chi, own, virtual, occupied = pl.pallas_call(
        functools.partial(chi_kernel, team, first, len(early), owners),
        out_shape=[jax.ShapeDtypeStruct((local_pairs, pair_count), jnp.float32), *prepared],
        in_specs=[IN_HBM] * 2 + [IN_VMEM] * (5 + len(early) + team),
        out_specs=[IN_VMEM] * 4,
        scratch_shapes=[pltpu.SemaphoreType.DMA((2,))],
        input_output_aliases={5: 1, 6: 2, 7: 3},
        compiler_params=params,
        cost_estimate=cost(bytes_accessed=2 * amplitudes.nbytes),
    )(
        in_hbm(amplitudes),
        in_hbm(integrals),
        *energies,
        *[near(array) for array in (own, virtual, occupied)],
        *early,
        *[near(far) for far in far_ints],
    )
    return pl.pallas_call(
        functools.partial(update_kernel, team, len(late), owners),
        out_shape=jax.ShapeDtypeStruct((local_pairs, width), jnp.bfloat16),
        in_specs=[IN_VMEM] * (3 + len(late) + team),
        out_specs=IN_HBM,
        scratch_shapes=[
            pltpu.VMEM((local_pairs, width), jnp.bfloat16),
            pltpu.SemaphoreType.DMA((IRREPS + 1,)),
        ],
        compiler_params=params,
        cost_estimate=cost(bytes_accessed=4 * local_pairs * width * 2),
    )(chi, virtual, occupied, *late, near(own), *[near(far) for far in far_amps])


def solution(mesh):
    size = mesh.shape["idx"]
    in_specs = (
        P(("grp", "idx"), None),
        P(("grp", "idx"), None),
        P(("grp", "idx"), None, None),
        P("grp"),
        P("grp"),
        P(("grp", "idx"), None),
    )
    out_specs = P(("grp", "idx"), None)

    def run(*args):
        return on_device(*args, size)

    return jax.shard_map(run, mesh=mesh, in_specs=in_specs, out_specs=out_specs, check_vma=False)
```
